128 devices in a mesh: row: 8 (over y, z_lo), col: 16 (over x, z_hi, core).
Axes of the slice: x: 4, y: 4, z: 4 (z_hi: 2, z_lo: 2; z = z_hi * 2 + z_lo), core: 2. Of those that a mesh axis runs over, the one named last changes fastest.
Arguments:
- slide_pixels: bfloat16 [3, 1024, 4096], P(None, 'row', 'col'), may hold values from -6 to 6
- stem_weight: bfloat16 [48, 96], replicated, may hold values from -0.875 to 0.875
- depth_kernel: float32 [96, 49], replicated, may hold values from -0.875 to 0.875
- expand_weight: bfloat16 [96, 384], replicated, may hold values from -0.625 to 0.625
- reduce_weight: bfloat16 [384, 96], replicated, may hold values from -0.3125 to 0.3125
- down_weight: bfloat16 [384, 192], replicated, may hold values from -0.3125 to 0.3125
- owner_weight: bfloat16 [8, 16, 192, 768], P('row', 'col'), may hold values from -0.4375 to 0.4375
- tissue_mask: int32 [16, 64], P('row', 'col'), may hold values 0 or 1
- owner_index: int32 [8, 128, 1], P('row', 'col'), may hold values from 0 to 15; in each aligned block of 8 rows (0 to 7, 8 to 15, ..., all dimensions but the last counted through in order) at most 2 rows name the same one
- patch_cotangent: bfloat16 [16, 64, 768], P('row', 'col'), may hold values from -6 to 6
Outputs:
- stem_grad: float32 [48, 96], replicated
- kernel_grad_out: float32 [96, 49], replicated
- expand_grad: float32 [96, 384], replicated
- reduce_grad: float32 [384, 96], replicated
- down_grad: float32 [384, 192], replicated
- owner_grad: float32 [8, 16, 192, 768], P('row', 'col')
The draws below stay inside these ranges and needn't reach their ends.
Inputs may be any that keep to these rules, and one draw needn't show every extreme that they name: `owner_index`: each device's 8 patch blocks name one owner at most 2 times, a bound that some block reaches.
All inputs are finite; a program needn't handle non-finite values. No bound on the sum of `tissue_mask` on one device may be relied on, other than what follows from the above.
Results may differ from the reference program's by a relative error of at most 0.014.
Values may be sent and summed in bfloat16 or wider, within the bound.
A program may use at most 128 MiB of HBM per device.

```python
import math
import jax
import jax.numpy as jnp
import numpy as np
from jax import lax

C0 = 96
C1 = 192
HID = 384
E = 768
PATCH = 64
CAP = 2
IMG_H = 1024
IMG_W = 4096
PB_H = 2
PB_W = 4
PBD = 8
GRID_H = 16
GRID_W = 64
N_ROW = 8
N_COL = 16


def place_ends(drawn, rng, low, high):
    extent = drawn.shape
    spot = [jax.random.randint(jax.random.fold_in(rng, axis), (), 0, extent[axis]) for axis in range(len(extent))]
    drawn = drawn.at[tuple(spot)].set(low)
    longest = extent.index(max(extent))
    spot[longest] = (spot[longest] + 1) % extent[longest]
    return drawn.at[tuple(spot)].set(high)


def block_levels(key, shape, split, smallest, high):
    gain, own = 1.0, jax.random.fold_in(key, 6)
    for position, parts in split:
        draws = jnp.exp(jax.random.uniform(jax.random.fold_in(own, position), (parts,), jnp.float32, smallest / len(split), high / len(split)))
        gain = gain * jnp.repeat(draws, shape[position] // parts).reshape([-1 if axis == position else 1 for axis in range(len(shape))])
    return gain


def routed_block(stream_key, own, number, rows, amount, top, most, slope):
    sequence = jax.random.permutation(stream_key, amount)
    heavy_load, ordinary = shares(amount, rows * top, most, slope, True), shares(amount, rows * top, most, slope, False)
    places = jnp.arange(amount)

    def named(tallies, turn):
        used = int((tallies > 0).sum())
        fixed = max(1, used // 4)
        shifted = fixed + (places - fixed + turn * (used - fixed)) % max(1, amount - fixed)
        return jnp.zeros((amount,), jnp.int32).at[sequence[jnp.where(places < fixed, places, shifted)]].set(jnp.asarray(tallies, jnp.int32))

    tallies = jnp.where(number % 4 == 0, named(heavy_load, number // 4), named(ordinary, number - number // 4 - 1))
    mixed = jax.random.permutation(jax.random.fold_in(own, 3), amount)
    source_of, taker = mixed[0:amount // 2 * 2:2], mixed[1:amount // 2 * 2:2]
    margin = jnp.minimum(tallies[source_of] - 1, most - tallies[taker]) // 2
    margin = jnp.where((source_of == sequence[0]) | (taker == sequence[0]) | (tallies[taker] == 0), 0, jnp.maximum(margin, 0))
    shifted = jax.random.randint(jax.random.fold_in(own, 4), (amount // 2,), 0, 1 << 20) % (margin + 1)
    tallies = tallies.at[source_of].add(-shifted).at[taker].add(shifted)
    items = jnp.searchsorted(jnp.cumsum(tallies), jnp.arange(rows * top), side="right").astype(jnp.int32)
    grid = items.reshape(top, rows).T
    grid = grid[jax.random.permutation(jax.random.fold_in(own, 1), rows)]
    turn = jax.random.randint(jax.random.fold_in(own, 2), (rows, 1), 0, top)
    return jnp.take_along_axis(grid, (jnp.arange(top)[None, :] + turn) % top, axis=1)


def shares(number_of, total, limit, skew, full):
    portions = [(1 << 20) // math.isqrt(rank ** skew) + 1 for rank in range(1, number_of + 1)]
    largest = limit if full else min(limit, max(-(-total // number_of), total * portions[0] // sum(portions)))
    least = 1 if total - largest >= number_of - 1 else 0
    given, spare = [largest] + [least] * (number_of - 1), total - largest - least * (number_of - 1)
    while spare > 0:
        movable = [i for i in range(1, number_of) if given[i] < largest] or [i for i in range(1, number_of) if given[i] < limit]
        mass, left = sum([portions[i] for i in movable]), spare
        for i in movable:
            more = min(limit - given[i], max(1, left * portions[i] // mass), spare)
            given[i] = given[i] + more
            spare = spare - more
    return np.array(given)


def scatter_about(stream_key, extent, deviation, most, pieces=(), held_as=jnp.bfloat16):
    drawn = deviation * jax.random.normal(stream_key, extent, jnp.float32)
    if pieces:
        drawn = drawn * block_levels(stream_key, extent, pieces, -0.22, 0.18)
    return jnp.clip(drawn, -most, most).astype(held_as)


def setup_inputs(seed: int = 0) -> dict:
    splits = jax.random.split(jax.random.key(seed), 11)
    slide_pixels = scatter_about(splits[0], (3, IMG_H, IMG_W), 1.0, 6.0, ((1, 8), (2, 16)))
    stem_weight = scatter_about(splits[1], (48, C0), 48 ** -0.5, 0.875)
    depth_kernel = scatter_about(splits[2], (C0, 49), 49 ** -0.5, 0.875, (), jnp.float32)
    expand_weight = scatter_about(splits[3], (C0, HID), C0 ** -0.5, 0.625)
    reduce_weight = scatter_about(splits[4], (HID, C0), HID ** -0.5, 0.3125)
    down_weight = scatter_about(splits[5], (4 * C0, C1), (4 * C0) ** -0.5, 0.3125)
    owner_weight = scatter_about(splits[6], (N_ROW, N_COL, C1, E), C1 ** -0.5, 0.4375, ((0, 8), (1, 16)))
    tissue_mask = place_ends((jax.random.randint(splits[7], (GRID_H, GRID_W), 0, 8) < 7).astype(jnp.int32), jax.random.fold_in(splits[7], 1), 0, 1)
    owner_index_keys = jax.random.split(jax.random.fold_in(splits[8], 1), N_ROW * (N_COL * PBD) // PBD)
    owner_index_turns = jax.random.permutation(jax.random.fold_in(splits[8], 3), N_ROW * (N_COL * PBD) // PBD)
    owner_index = jax.vmap(lambda own, number: routed_block(jax.random.fold_in(splits[8], 2), own, number, PBD, N_COL, 1, CAP, 2))(owner_index_keys, owner_index_turns).reshape((N_ROW, N_COL * PBD, 1))
    patch_cotangent = scatter_about(splits[9], (GRID_H, GRID_W, E), 1.0, 6.0, ((0, 8), (1, 16)))
    return {"slide_pixels": slide_pixels, "stem_weight": stem_weight, "depth_kernel": depth_kernel, "expand_weight": expand_weight, "reduce_weight": reduce_weight, "down_weight": down_weight, "owner_weight": owner_weight, "tissue_mask": tissue_mask, "owner_index": owner_index, "patch_cotangent": patch_cotangent}


epsilon = 1e-06
slope_factor = 0.7978845608028654
cubic_factor = 0.044715

def channel_norm(values, axis):
    center = values - lax.optimization_barrier(jnp.mean(values, axis=axis, keepdims=True))
    scale = lax.rsqrt(lax.optimization_barrier(jnp.mean(center * center, axis=axis, keepdims=True)) + epsilon)
    return (center * scale, scale)

def norm_back(normed, scale, grad, axis):
    return scale * (grad - lax.optimization_barrier(jnp.mean(grad, axis=axis, keepdims=True)) - normed * lax.optimization_barrier(jnp.mean(grad * normed, axis=axis, keepdims=True)))

def gelu_value(hidden):
    return 0.5 * hidden * (1.0 + jnp.tanh(slope_factor * (hidden + cubic_factor * hidden * hidden * hidden)))

def gelu_slope(hidden):
    tangent = jnp.tanh(slope_factor * (hidden + cubic_factor * hidden * hidden * hidden))
    return 0.5 * (1.0 + tangent) + 0.5 * hidden * (1.0 - tangent * tangent) * slope_factor * (1.0 + 3.0 * cubic_factor * hidden * hidden)

def patchify(pixels):
    channels, height, width = pixels.shape
    blocks = pixels.reshape(channels, height // 4, 4, width // 4, 4)
    return blocks.transpose(0, 2, 4, 1, 3).reshape(channels * 16, height // 4, width // 4)

def depthwise(padded, kernel, height, width):
    total = jnp.zeros((padded.shape[0], height, width), jnp.float32)
    for row_off in range(7):
        for col_off in range(7):
            tap = kernel[:, row_off * 7 + col_off][:, None, None]
            total = total + tap * padded[:, row_off:row_off + height, col_off:col_off + width]
    return total

def kernel_taps(padded, grad, height, width):
    taps = []
    for row_off in range(7):
        for col_off in range(7):
            taps.append(lax.optimization_barrier(jnp.sum(grad * padded[:, row_off:row_off + height, col_off:col_off + width], axis=(1, 2))))
    return jnp.stack(taps, axis=1)

def conv_back(grad_padded, kernel, height, width):
    total = jnp.zeros((grad_padded.shape[0], height, width), jnp.float32)
    for row_off in range(7):
        for col_off in range(7):
            tap = kernel[:, row_off * 7 + col_off][:, None, None]
            total = total + tap * grad_padded[:, 6 - row_off:6 - row_off + height, 6 - col_off:6 - col_off + width]
    return total

def owner_work(cells, cot_scaled, weight, patch_side):
    normed, scale = channel_norm(cells.astype(jnp.float32), 1)
    normed_b = normed.astype(jnp.bfloat16).astype(jnp.float32)
    weight_f = weight.astype(jnp.float32)
    if weight.ndim == 2:
        token_pre = jnp.einsum('ke,skt->set', weight_f, normed_b)
    else:
        token_pre = jnp.einsum('ske,skt->set', weight_f, normed_b)
    pre_grad = (cot_scaled[:, :, None] / patch_side * gelu_slope(token_pre)).astype(jnp.bfloat16).astype(jnp.float32)
    if weight.ndim == 2:
        weight_grad = jnp.einsum('skt,set->ke', normed_b, pre_grad)
        normed_grad = jnp.einsum('ke,set->skt', weight_f, pre_grad)
    else:
        weight_grad = jnp.einsum('skt,set->ske', normed_b, pre_grad)
        normed_grad = jnp.einsum('ske,set->skt', weight_f, pre_grad)
    cells_grad = norm_back(normed, scale, normed_grad, 1).astype(jnp.bfloat16)
    return (cells_grad, weight_grad)

def split_blocks(values, count):
    return values.reshape(values.shape[0], count, -1).transpose(1, 0, 2)

def join_blocks(blocks):
    return blocks.transpose(1, 0, 2).reshape(blocks.shape[1], -1)

def reference(slide_pixels, stem_weight, depth_kernel, expand_weight, reduce_weight, down_weight, owner_weight, tissue_mask, owner_index, patch_cotangent):
    loss_scale = (N_ROW * N_COL) ** (-0.5)
    patch_side = PATCH // 8
    pixel_blocks = patchify(slide_pixels)
    cell_h, cell_w = (pixel_blocks.shape[1], pixel_blocks.shape[2])
    flat_blocks = pixel_blocks.reshape(48, cell_h * cell_w)
    stem_pre = jnp.dot(stem_weight.T, flat_blocks, preferred_element_type=jnp.float32)
    stem_norm, stem_scale = channel_norm(stem_pre, 0)
    stem_out = stem_norm.astype(jnp.bfloat16).astype(jnp.float32)
    stem_grid = stem_out.reshape(C0, cell_h, cell_w)
    padded = jnp.pad(stem_grid, ((0, 0), (3, 3), (3, 3)))
    depth_out = depthwise(padded, depth_kernel, cell_h, cell_w).reshape(C0, cell_h * cell_w)
    mixed_norm, mixed_scale = channel_norm(depth_out, 0)
    mixed = mixed_norm.astype(jnp.bfloat16)

    def mlp_forward(block):
        hidden_pre = jnp.dot(expand_weight.T, block, preferred_element_type=jnp.float32)
        activated = gelu_value(hidden_pre).astype(jnp.bfloat16)
        return jnp.dot(reduce_weight.T, activated, preferred_element_type=jnp.float32)
    branch = join_blocks(lax.map(mlp_forward, split_blocks(mixed, N_ROW)))
    block_out = stem_out + branch
    down_norm, down_scale = channel_norm(block_out, 0)
    down_in = down_norm.astype(jnp.bfloat16)
    down_h, down_w = (cell_h // 2, cell_w // 2)
    grouped = down_in.reshape(C0, down_h, 2, down_w, 2).transpose(2, 4, 0, 1, 3).reshape(4 * C0, down_h * down_w)
    embed = jnp.dot(down_weight.T, grouped, preferred_element_type=jnp.float32).astype(jnp.bfloat16)
    grid_h, grid_w = (down_h // patch_side, down_w // patch_side)
    patch_cells = embed.reshape(C1, grid_h, patch_side, grid_w, patch_side).transpose(1, 3, 0, 2, 4).reshape(grid_h * grid_w, C1, patch_side * patch_side)
    owners = owner_index.reshape(N_ROW, N_COL, PB_H, PB_W).transpose(0, 2, 1, 3).reshape(-1).astype(jnp.int32)
    mesh_rows = jnp.repeat(jnp.arange(grid_h, dtype=jnp.int32) // PB_H, grid_w).astype(jnp.int32)
    cot_scaled = patch_cotangent.astype(jnp.float32).reshape(-1, E) * tissue_mask.reshape(-1, 1).astype(jnp.float32) * loss_scale

    def owner_step(carry, inputs):
        cells, cotangent, row_id, dest = inputs
        weight = owner_weight[row_id, dest]
        cells_grad, weight_grad = owner_work(cells[None], cotangent[None], weight, patch_side)
        return (carry.at[row_id, dest].add(weight_grad), cells_grad[0])
    start_grad = jnp.zeros((N_ROW, N_COL, C1, E), jnp.float32)
    owner_grad, embed_grad = lax.scan(owner_step, start_grad, (patch_cells, cot_scaled, mesh_rows, owners))
    embed_grad = embed_grad.reshape(grid_h, grid_w, C1, patch_side, patch_side).transpose(2, 0, 3, 1, 4).reshape(C1, down_h * down_w)
    down_grad = jnp.dot(grouped, embed_grad.T, preferred_element_type=jnp.float32)
    group_back = jnp.dot(down_weight, embed_grad, preferred_element_type=jnp.float32)
    group_back = group_back.reshape(2, 2, C0, down_h, down_w).transpose(2, 3, 0, 4, 1).reshape(C0, cell_h * cell_w)
    block_grad = norm_back(down_norm, down_scale, group_back, 0)

    def mlp_backward(inputs):
        block, grad = inputs
        hidden_pre = jnp.dot(expand_weight.T, block, preferred_element_type=jnp.float32)
        activated = gelu_value(hidden_pre).astype(jnp.bfloat16)
        out_grad = grad.astype(jnp.bfloat16)
        reduce_part = jnp.dot(activated, out_grad.T, preferred_element_type=jnp.float32)
        act_grad = jnp.dot(reduce_weight, out_grad, preferred_element_type=jnp.float32)
        hid_grad = (act_grad * gelu_slope(hidden_pre)).astype(jnp.bfloat16)
        expand_part = jnp.dot(block, hid_grad.T, preferred_element_type=jnp.float32)
        mixed_grad = jnp.dot(expand_weight, hid_grad, preferred_element_type=jnp.float32)
        return (mixed_grad, expand_part, reduce_part)
    mixed_grads, expand_parts, reduce_parts = lax.map(mlp_backward, (split_blocks(mixed, N_ROW), split_blocks(block_grad, N_ROW)))
    mixed_grad = join_blocks(mixed_grads)
    expand_grad = lax.optimization_barrier(jnp.sum(expand_parts, axis=0))
    reduce_grad = lax.optimization_barrier(jnp.sum(reduce_parts, axis=0))
    depth_grad = norm_back(mixed_norm, mixed_scale, mixed_grad, 0).reshape(C0, cell_h, cell_w)
    kernel_grad_out = kernel_taps(padded, depth_grad, cell_h, cell_w)
    grad_padded = jnp.pad(depth_grad, ((0, 0), (3, 3), (3, 3)))
    stem_in_grad = block_grad + conv_back(grad_padded, depth_kernel, cell_h, cell_w).reshape(C0, cell_h * cell_w)
    pre_grad_stem = norm_back(stem_norm, stem_scale, stem_in_grad, 0).astype(jnp.bfloat16)
    stem_grad = jnp.dot(flat_blocks, pre_grad_stem.T, preferred_element_type=jnp.float32)
    return (stem_grad, kernel_grad_out, expand_grad, reduce_grad, down_grad, owner_grad)
```

```python
import jax
import jax.numpy as jnp
from jax import lax
from jax.experimental import pallas as pl
from jax.experimental.pallas import tpu as pltpu
from jax.sharding import PartitionSpec as P

C0, C1, HID, E = 96, 192, 384, 768
ROWS, COLS = 8, 16
BF, F32, I32 = jnp.bfloat16, jnp.float32, jnp.int32
EPS = 1e-06
SLOPE = 0.7978845608028654
CUBIC = 0.044715
MESH = pl.DeviceIdType.MESH
NEAR = ((-1, 0), (1, 0), (0, -1), (0, 1), (-1, -1), (-1, 1), (1, -1), (1, 1))

NN = (((1,), (0,)), ((), ()))
NT = (((1,), (1,)), ((), ()))
TN = (((0,), (0,)), ((), ()))


def dot(a, b, dims=NN):
    return lax.dot_general(a, b, dims, preferred_element_type=F32)


def iota(shape, dim):
    return lax.broadcasted_iota(I32, shape, dim)


def norm_lanes(x, mask):
    mean = jnp.sum(x, axis=-1, keepdims=True) * (1.0 / C0)
    center = (x - mean) * mask
    scale = lax.rsqrt(jnp.sum(center * center, axis=-1, keepdims=True) * (1.0 / C0) + EPS)
    return center * scale, scale


def norm_back_lanes(normed, scale, grad):
    mean = jnp.sum(grad, axis=-1, keepdims=True) * (1.0 / C0)
    proj = jnp.sum(grad * normed, axis=-1, keepdims=True) * (1.0 / C0)
    return scale * (grad - mean - normed * proj)


def gelu_both(h):
    sq = h * h
    t = jnp.tanh(SLOPE * h * (1.0 + CUBIC * sq))
    half = 0.5 * (1.0 + t)
    return h * half, half + 0.5 * h * (1.0 - t * t) * (SLOPE * (1.0 + 3.0 * CUBIC * sq))


def depthwise(src, kb, dst, flip):
    def body(n, carry):
        ib, jb = n // 8, n % 8
        i0 = ib * 8
        acc = [None] * 8
        for v in range(7):
            taps = []
            for u in range(7):
                tap = 7 * u + v
                taps.append(kb[48 - tap if flip else tap])
            for r in range(14):
                x = src[i0 + r + 1, pl.ds(jb * 8 + v, 8), :]
                for u in range(7):
                    i = r - u
                    if 0 <= i < 8:
                        term = taps[u] * x
                        acc[i] = term if acc[i] is None else acc[i] + term
        for i in range(8):
            dst[i0 + i, pl.ds(pl.multiple_of(jb * 8, 8), 8), :] = acc[i]
        return carry

    lax.fori_loop(0, 32, body, 0)


def kernel(
    pix, ws, dk, we, wr, wd, wo, tissue, owners, cot,
    out_stem, out_taps, out_expand, out_reduce, out_down, out_owner,
    xe, perm, permi, wblk, ws128, dkp, kb, we128, wr128, dwp, dwt,
    pad, sn, ss, ft, conv, mn, ms, mb, act, slope, dn, ds, gp, pmt,
    cots, sbuf, rbuf, rets, ret, wt, gs, dgu, dgp, hrow, hcol, hcor,
    acc_s, acc_e, acc_r,
    g1, g1r1, g1p2, g1r2, g1p3, g1a, g2, g2r1, g2p2, g2r2, g2p3, g2a,
    px_s, px_r, a_s, a_r, b_s, b_r, h_s, h_r,
    p1_s, p1_r, p2_s, p2_r, p3_s, p3_r, q1_s, q1_r, q2_s, q2_r, q3_s, q3_r,
):
    row, col = lax.axis_index("row"), lax.axis_index("col")

    def near(n):
        dr, dc = NEAR[n]
        return lax.rem(row + (dr + ROWS), ROWS), lax.rem(col + (dc + COLS), COLS)

    def col_peer(k):
        return row, lax.rem(col + k, COLS)

    def row_peer(k):
        return lax.rem(row + k, ROWS), col

    def remote(src, dst, send, recv, dev):
        return pltpu.make_async_remote_copy(
            src_ref=src, dst_ref=dst, send_sem=send, recv_sem=recv, device_id=dev, device_id_type=MESH
        )

    barrier = pltpu.get_barrier_semaphore()
    for k in range(1, COLS):
        pl.semaphore_signal(barrier, inc=1, device_id=col_peer(k), device_id_type=MESH)
    for k in range(1, ROWS):
        pl.semaphore_signal(barrier, inc=1, device_id=row_peer(k), device_id_type=MESH)
    for n in range(4, 8):
        pl.semaphore_signal(barrier, inc=1, device_id=near(n), device_id_type=MESH)
    pl.semaphore_wait(barrier, (COLS - 1) + (ROWS - 1) + 4)

    px_src = (
        pix.at[:, 0:16, :], pix.at[:, 112:128, :], pix.at[:, :, 0:128], pix.at[:, :, 128:256],
        pix.at[:, 0:16, 0:128], pix.at[:, 0:16, 128:256], pix.at[:, 112:128, 0:128], pix.at[:, 112:128, 128:256],
    )
    px_dst = (
        xe.at[:, 144:160, 128:384], xe.at[:, 0:16, 128:384], xe.at[:, 16:144, 384:512], xe.at[:, 16:144, 0:128],
        xe.at[:, 144:160, 384:512], xe.at[:, 144:160, 0:128], xe.at[:, 0:16, 384:512], xe.at[:, 0:16, 0:128],
    )
    px = [remote(px_src[n], px_dst[n], px_s.at[n], px_r.at[n], near(n)) for n in range(8)]
    for n in range(8):
        px[n].start()

    mask = (iota((1, 128), 1) < C0).astype(F32)
    xe[:, 16:144, 128:384] = pix[...]
    pr = iota((288, 512), 0)
    perm[...] = (iota((288, 512), 1) == 116 + 4 * (pr % 72) + pr // 72).astype(F32).astype(BF)
    for s in range(4):
        permi[s] = (iota((256, 64), 0) == 4 * iota((256, 64), 1) + s).astype(F32).astype(BF)
    ws128[...] = jnp.zeros_like(ws128)
    ws128[:, 0:C0] = ws[...]
    q48 = iota((48, 48), 0)
    ql = iota((48, 128), 0)
    for s in range(4):
        pick = (iota((48, 48), 1) == (q48 // 16) * 16 + (q48 % 4) * 4 + s).astype(F32).astype(BF)
        wsel = dot(pick, ws128[...])
        for i4 in range(4):
            wblk[s, :, i4 * 128 : (i4 + 1) * 128] = jnp.where((ql // 4) % 4 == i4, wsel, 0.0).astype(BF)
    dkp[...] = jnp.zeros_like(dkp)
    dkp[0:C0, 0:49] = dk[...]
    dkt = dkp[...].T
    for t in range(49):
        kb[t] = jnp.broadcast_to(dkt[t : t + 1, :], (8, 128))
    we128[...] = jnp.zeros_like(we128)
    we128[0:C0, :] = we[...]
    wr128[...] = jnp.zeros_like(wr128)
    wr128[:, 0:C0] = wr[...]
    dwp[...] = jnp.zeros_like(dwp)
    for b in range(4):
        dwp[b * 128 : b * 128 + C0, :] = wd[b * C0 : (b + 1) * C0, :]
    dwt[...] = dwp[...].astype(F32).T.astype(BF)
    wt[...] = wo[0, 0].astype(F32).T.astype(BF)

    slots = []
    for p in range(8):
        rank = 0
        for q in range(p):
            same = jnp.where(owners[0, q, 0] == owners[0, p, 0], 1, 0)
            rank = rank + same * tissue[q // 4, q % 4]
        slots.append(jnp.where(tissue[p // 4, p % 4] == 1, owners[0, p, 0] * 2 + rank, -1000))
    rr = iota((512, 128), 0)
    ll = iota((512, 128), 1)
    patch = (rr // 256) * 4 + (rr % 32) // 8
    slot_row = jnp.zeros((512, 128), I32)
    for p in range(8):
        slot_row = jnp.where(patch == p, slots[p], slot_row)
    hit = jnp.where(((rr // 32) % 8) * 8 + rr % 8 == ll % 64, slot_row - ll // 64, -2000)
    for d in range(COLS):
        pmt[:, d * 128 : (d + 1) * 128] = (hit == 2 * d).astype(F32).astype(BF)
    cots[...] = jnp.zeros_like(cots)
    cots[0:4, :] = cot[0].astype(F32)
    cots[4:8, :] = cot[1].astype(F32)
    slot_lane = jnp.full((256, 16), -1000, I32)
    for p in range(8):
        slot_lane = jnp.where(iota((256, 16), 1) == p, slots[p], slot_lane)
    ro = iota((256, 16), 0)
    rem16 = ro % 16
    want = jnp.where(rem16 < 12, 2 * (ro // 16) + rem16 // 6, -3000)
    packed = jnp.zeros((256, 128), F32)
    for b in range(6):
        choose = jnp.where(rem16 % 6 == b, want, -3000)
        packed = packed + dot(
            (slot_lane == choose).astype(F32).astype(BF), cots[:, b * 128 : (b + 1) * 128].astype(BF)
        )
    for d in range(COLS):
        sbuf[d, C1 : C1 + 16, :] = packed[d * 16 : (d + 1) * 16].astype(BF)

    for n in range(8):
        px[n].wait_recv()

    @pl.when(row == 0)
    def _():
        xe[:, 0:16, :] = jnp.zeros((3, 16, 512), BF)

    @pl.when(row == ROWS - 1)
    def _():
        xe[:, 144:160, :] = jnp.zeros((3, 16, 512), BF)

    @pl.when(col == 0)
    def _():
        xe[:, :, 0:128] = jnp.zeros((3, 160, 128), BF)

    @pl.when(col == COLS - 1)
    def _():
        xe[:, :, 384:512] = jnp.zeros((3, 160, 128), BF)

    def stem_body(g, carry):
        at = pl.ds(pl.multiple_of(g * 16, 16), 16)
        xg = jnp.concatenate([xe[0, at, :], xe[1, at, :], xe[2, at, :]], axis=0)
        turned = dot(perm[...], xg, NT)
        total = jnp.zeros((72, 512), F32)
        for s in range(4):
            total = total + dot(turned[s * 72 : (s + 1) * 72].astype(BF), wblk[s])
        for i4 in range(4):
            normed, scale = norm_lanes(total[:, i4 * 128 : (i4 + 1) * 128], mask)
            pad[4 * g + i4] = normed.astype(BF).astype(F32)
            sn[4 * g + i4] = normed
            ss[4 * g + i4] = jnp.broadcast_to(scale, (72, 128))
        return carry

    lax.fori_loop(0, 10, stem_body, 0)

    def flat_body(g, carry):
        at = pl.ds(pl.multiple_of(g * 16 + 16, 16), 16)
        xg = jnp.concatenate([xe[0, at, 128:384], xe[1, at, 128:384], xe[2, at, 128:384]], axis=0)
        for s in range(4):
            ft[g, s * 48 : (s + 1) * 48, :] = dot(xg, permi[s]).astype(BF)
        return carry

    lax.fori_loop(0, 8, flat_body, 0)

    depthwise(pad, kb, conv, False)

    def mlp_body(b, carry):
        rows4 = pl.ds(b * 4, 4)
        rows = pl.ds(pl.multiple_of(b * 256, 256), 256)
        normed, scale = norm_lanes(conv[rows4].reshape(256, 128), mask)
        mn[rows, :] = normed
        ms[rows, :] = jnp.broadcast_to(scale, (256, 128))
        mixed = normed.astype(BF)
        mb[rows, :] = mixed
        value, grad = gelu_both(dot(mixed, we128[...]))
        value = value.astype(BF)
        act[rows, :] = value
        slope[rows, :] = grad.astype(BF)
        block = jnp.concatenate([pad[b * 4 + 4 + i, 3:67, :] for i in range(4)], axis=0)
        block = block + dot(value, wr128[...])
        normed, scale = norm_lanes(block, mask)
        dn[rows4] = normed.reshape(4, 64, 128)
        ds[rows, :] = jnp.broadcast_to(scale, (256, 128))
        return carry

    lax.fori_loop(0, 8, mlp_body, 0)

    def group_body(i, carry):
        rows = pl.ds(pl.multiple_of(i * 32, 32), 32)
        for u in range(2):
            for v in range(2):
                b = 2 * u + v
                gp[rows, b * 128 : (b + 1) * 128] = dn[2 * i + u, pl.ds(v, 32, stride=2), :].astype(BF)
        return carry

    lax.fori_loop(0, 16, group_body, 0)
    embed = dot(dwt[...], gp[...], NT).astype(BF)

    for d in range(COLS):
        sbuf[d, 0:C1, :] = dot(embed, pmt[:, d * 128 : (d + 1) * 128]).astype(BF)
    outs = []
    for k in range(1, COLS):
        peer = col_peer(k)
        cp = remote(sbuf.at[peer[1]], rbuf.at[k], a_s.at[k], a_r.at[k], peer)
        cp.start()
        outs.append(cp)

    out_owner[0, 0] = jnp.zeros((C1, E), F32)
    sel = (iota((16, E), 0) == ((iota((16, E), 1) % 128) // 64) * 6 + iota((16, E), 1) // 128).astype(F32).astype(BF)
    cot_scale = (ROWS * COLS) ** (-0.5) / 8.0

    def own(load):
        cells = load(0, C1).astype(F32)
        mean = jnp.sum(cells, axis=0, keepdims=True) * (1.0 / C1)
        center = cells - mean
        scale = lax.rsqrt(jnp.sum(center * center, axis=0, keepdims=True) * (1.0 / C1) + EPS)
        normed = center * scale
        nb = normed.astype(BF)
        cott = dot(load(C1, 16), sel, TN) * cot_scale
        back = jnp.zeros((C1, 128), F32)
        for b in range(6):
            lanes = slice(b * 128, (b + 1) * 128)
            pre = dot(wt[lanes, :], nb)
            pg = (cott[:, lanes] * gelu_both(pre)[1]).astype(BF)
            out_owner[0, 0, :, lanes] += dot(nb, pg, NT)
            back = back + dot(wo[0, 0, :, lanes], pg)
        mean = jnp.sum(back, axis=0, keepdims=True) * (1.0 / C1)
        proj = jnp.sum(back * normed, axis=0, keepdims=True) * (1.0 / C1)
        return (scale * (back - mean - normed * proj)).astype(BF)

    mine = pl.ds(pl.multiple_of(col * 128, 128), 128)

    def back_copy(k):
        dev = (row, lax.rem(col - k + COLS, COLS))
        return remote(rets.at[k], ret.at[:, mine], b_s.at[k], b_r.at[k], dev)

    ret[:, mine] = own(lambda a, n: sbuf[col, a : a + n, :])

    def own_body(k, carry):
        remote(sbuf.at[k], rbuf.at[k], a_s.at[k], a_r.at[k], col_peer(k)).wait_recv()
        rets[k] = own(lambda a, n: rbuf[k, a : a + n, :])
        back_copy(k).start()
        return carry

    lax.fori_loop(1, COLS, own_body, 0)
    for k in range(1, COLS):
        outs[k - 1].wait_send()

    for k in range(1, COLS):
        back_copy(k).wait_recv()
    eg = dot(ret[...], pmt[...], NT).astype(BF)
    egt = dot(pmt[...], ret[...], NT).astype(BF)

    for b in range(4):
        lanes = slice(b * 128, (b + 1) * 128)
        part = dot(eg, gp[:, lanes]).astype(BF)
        g1[6 + 2 * b] = part[0:96]
        g1[7 + 2 * b] = part[96:192]

    gb = dot(egt, dwt[...])
    for i in range(16):
        for b in range(4):
            gs[2 * i + b // 2, pl.ds(b % 2, 32, stride=2), :] = gb[i * 32 : (i + 1) * 32, b * 128 : (b + 1) * 128]

    acc_e[...] = jnp.zeros_like(acc_e)
    acc_r[...] = jnp.zeros_like(acc_r)

    def back_body(b, carry):
        rows4 = pl.ds(b * 4, 4)
        rows = pl.ds(pl.multiple_of(b * 256, 256), 256)
        grad = gs[rows4].reshape(256, 128)
        grad = norm_back_lanes(dn[rows4].reshape(256, 128), ds[rows, :], grad) * mask
        gs[rows4] = grad.reshape(4, 64, 128)
        og = grad.astype(BF)
        acc_r[...] += dot(og, act[rows, :], TN)
        hid = (dot(og, wr128[...], NT) * slope[rows, :].astype(F32)).astype(BF)
        acc_e[...] += dot(mb[rows, :], hid, TN)
        mg = dot(hid, we128[...], NT)
        dg = norm_back_lanes(mn[rows, :], ms[rows, :], mg) * mask
        dgu[rows4] = dg.reshape(4, 64, 128)
        return carry

    lax.fori_loop(0, 8, back_body, 0)

    h_src = (
        dgu.at[0:3], dgu.at[29:32], dgu.at[:, 0:8, :], dgu.at[:, 56:64, :],
        dgu.at[0:3, 0:8, :], dgu.at[0:3, 56:64, :], dgu.at[29:32, 0:8, :], dgu.at[29:32, 56:64, :],
    )
    h_dst = (
        hrow.at[1], hrow.at[0], hcol.at[1], hcol.at[0], hcor.at[3], hcor.at[2], hcor.at[1], hcor.at[0],
    )
    halo = [remote(h_src[n], h_dst[n], h_s.at[n], h_r.at[n], near(n)) for n in range(8)]
    for n in range(8):
        halo[n].start()

    for b in range(3):
        lanes = slice(b * 128, (b + 1) * 128)
        g1[b] = acc_e[0:C0, lanes].astype(BF)
        g1[3 + b] = acc_r[0:C0, lanes].astype(BF)
    g1[14] = jnp.zeros((96, 128), BF)
    g1[15] = jnp.zeros((96, 128), BF)

    def make_sum(g, r1, p2, r2, p3, ga, s1, t1, s2, t2, s3, t3):
        first = [
            remote(g.at[col_peer(k)[1]], r1.at[k], s1.at[k], t1.at[k], col_peer(k)) for k in range(1, COLS)
        ]
        second = [remote(p2, r2.at[row], s2.at[k], t2.at[k], row_peer(k)) for k in range(1, ROWS)]
        third = [remote(p3, ga.at[col], s3.at[k], t3.at[k], col_peer(k)) for k in range(1, COLS)]

        def start():
            for cp in first:
                cp.start()

        def turn():
            for cp in first:
                cp.wait_recv()
            total = g[col].astype(F32)
            for k in range(1, COLS):
                total = total + r1[k].astype(F32)
            p2[...] = total.astype(p2.dtype)
            r2[row] = total.astype(p2.dtype)
            for cp in second:
                cp.start()

        def spread():
            for cp in second:
                cp.wait_recv()
            total = r2[0].astype(F32)
            for k in range(1, ROWS):
                total = total + r2[k].astype(F32)
            p3[...] = total.astype(p3.dtype)
            ga[col] = total.astype(p3.dtype)
            for cp in third:
                cp.start()

        def finish():
            for cp in third:
                cp.wait_recv()

        def drain():
            for cp in first + second + third:
                cp.wait_send()

        return start, turn, spread, finish, drain

    start1, turn1, spread1, finish1, drain1 = make_sum(
        g1, g1r1, g1p2, g1r2, g1p3, g1a, p1_s, p1_r, p2_s, p2_r, p3_s, p3_r
    )
    start2, turn2, spread2, finish2, drain2 = make_sum(
        g2, g2r1, g2p2, g2r2, g2p3, g2a, q1_s, q1_r, q2_s, q2_r, q3_s, q3_r
    )
    start1()

    g2[...] = jnp.zeros_like(g2)
    for v in range(7):

        def taps_body(jb, acc, v=v):
            acc = list(acc)
            here = pl.ds(pl.multiple_of(jb * 8, 8), 8)
            grads = {}
            for r in range(38):
                x = pad[r + 1, pl.ds(jb * 8 + v, 8), :]
                if r < 32:
                    grads[r] = dgu[r, here, :]
                for u in range(7):
                    if 0 <= r - u < 32:
                        acc[u] = acc[u] + grads[r - u] * x
            return tuple(acc)

        sums = lax.fori_loop(0, 8, taps_body, tuple(jnp.zeros((8, 128), F32) for _ in range(7)))
        for u in range(7):
            at = 48 + 7 * u + v
            g2[at // 8, at % 8 : at % 8 + 1, :] = jnp.sum(sums[u], axis=0, keepdims=True)

    turn1()

    dgp[...] = jnp.zeros_like(dgp)
    for i in range(32):
        dgp[4 + i, 3:67, :] = dgu[i]
    for n in range(8):
        halo[n].wait_recv()
    top, bottom = jnp.where(row > 0, 1.0, 0.0), jnp.where(row < ROWS - 1, 1.0, 0.0)
    left, right = jnp.where(col > 0, 1.0, 0.0), jnp.where(col < COLS - 1, 1.0, 0.0)
    for i in range(3):
        dgp[1 + i, 3:67, :] = hrow[0, i] * top
        dgp[36 + i, 3:67, :] = hrow[1, i] * bottom
        dgp[1 + i, 0:3, :] = hcor[0, i, 5:8] * (top * left)
        dgp[1 + i, 67:70, :] = hcor[1, i, 0:3] * (top * right)
        dgp[36 + i, 0:3, :] = hcor[2, i, 5:8] * (bottom * left)
        dgp[36 + i, 67:70, :] = hcor[3, i, 0:3] * (bottom * right)
    dgp[4:36, 0:3, :] = hcol[0, :, 5:8, :] * left
    dgp[4:36, 67:70, :] = hcol[1, :, 0:3, :] * right

    depthwise(dgp, kb, conv, True)
    spread1()

    acc_s[...] = jnp.zeros_like(acc_s)

    def stem_back(g, carry):
        parts = []
        for i in range(4):
            grad = gs[4 * g + i] + conv[4 * g + i]
            parts.append(
                norm_back_lanes(sn[4 * g + 4 + i, 3:67, :], ss[4 * g + 4 + i, 3:67, :], grad).astype(BF)
            )
        grads = jnp.concatenate(parts, axis=1)
        for s in range(4):
            acc_s[s * 48 : (s + 1) * 48, :] += dot(ft[g, s * 48 : (s + 1) * 48, :], grads)
        return carry

    lax.fori_loop(0, 8, stem_back, 0)
    rows = iota((192, 128), 0)
    folded = jnp.zeros((192, 128), F32)
    for i4 in range(4):
        folded = folded + jnp.where((rows // 4) % 4 == i4, acc_s[:, i4 * 128 : (i4 + 1) * 128], 0.0)
    m48, q192 = iota((48, 192), 0), iota((48, 192), 1)
    rem = q192 % 48
    gather = (m48 == (rem // 16) * 16 + (rem % 4) * 4 + q192 // 48).astype(F32)
    stem = lax.dot_general(gather, folded, NN, precision=lax.Precision.HIGHEST, preferred_element_type=F32)
    for n in range(6):
        g2[n] = stem[n * 8 : (n + 1) * 8]

    start2()
    finish1()
    for b in range(3):
        lanes = slice(b * 128, (b + 1) * 128)
        out_expand[:, lanes] = g1a[b].astype(F32)
        out_reduce[lanes, :] = g1a[3 + b].astype(F32).T
    for b in range(4):
        out_down[b * C0 : (b + 1) * C0, 0:96] = g1a[6 + 2 * b].astype(F32).T[0:C0, :]
        out_down[b * C0 : (b + 1) * C0, 96:192] = g1a[7 + 2 * b].astype(F32).T[0:C0, :]
    turn2()
    spread2()
    finish2()
    for n in range(6):
        out_stem[n * 8 : (n + 1) * 8, :] = g2a[n, :, 0:C0]
    for n in range(6, 16):
        dkp[(n - 6) * 8 : (n - 5) * 8, :] = g2a[n]
    out_taps[...] = dkp[...].T[0:C0, 0:49]

    for n in range(8):
        px[n].wait_send()
        halo[n].wait_send()
    for k in range(1, COLS):
        back_copy(k).wait_send()
    drain1()
    drain2()


def on_device(pixels, ws, dk, we, wr, wd, wo, tissue, owners, cot):
    vmem = pl.BlockSpec(memory_space=pltpu.VMEM)
    smem = pl.BlockSpec(memory_space=pltpu.SMEM)
    dma = pltpu.SemaphoreType.DMA
    V = pltpu.VMEM
    outs = ((48, C0), (C0, 49), (C0, HID), (HID, C0), (4 * C0, C1), (1, 1, C1, E))
    return pl.pallas_call(
        kernel,
        out_shape=tuple(jax.ShapeDtypeStruct(s, F32) for s in outs),
        in_specs=[vmem] * 7 + [smem, smem, vmem],
        out_specs=(vmem,) * 6,
        scratch_shapes=[
            V((3, 160, 512), BF), V((288, 512), BF), V((4, 256, 64), BF), V((4, 48, 512), BF), V((48, 128), BF),
            V((128, 128), F32), V((49, 8, 128), F32), V((128, HID), BF), V((HID, 128), BF),
            V((512, C1), BF), V((C1, 512), BF),
            V((40, 72, 128), F32), V((40, 72, 128), F32), V((40, 72, 128), F32), V((8, 192, 64), BF),
            V((32, 64, 128), F32), V((2048, 128), F32), V((2048, 128), F32), V((2048, 128), BF),
            V((2048, HID), BF), V((2048, HID), BF), V((32, 64, 128), F32), V((2048, 128), F32),
            V((512, 512), BF), V((512, 2048), BF),
            V((16, E), F32), V((16, 208, 128), BF), V((16, 208, 128), BF), V((16, C1, 128), BF), V((C1, 2048), BF),
            V((E, C1), BF), V((32, 64, 128), F32), V((32, 64, 128), F32), V((40, 72, 128), F32),
            V((2, 3, 64, 128), F32), V((2, 32, 8, 128), F32), V((4, 3, 8, 128), F32),
            V((192, 512), F32), V((128, HID), F32), V((128, HID), F32),
            V((16, 96, 128), BF), V((16, 96, 128), BF), V((96, 128), BF), V((8, 96, 128), BF), V((96, 128), BF),
            V((16, 96, 128), BF),
            V((16, 8, 128), F32), V((16, 8, 128), F32), V((8, 128), F32), V((8, 8, 128), F32), V((8, 128), F32),
            V((16, 8, 128), F32),
            dma((8,)), dma((8,)), dma((16,)), dma((16,)), dma((16,)), dma((16,)), dma((8,)), dma((8,)),
            dma((16,)), dma((16,)), dma((8,)), dma((8,)), dma((16,)), dma((16,)),
            dma((16,)), dma((16,)), dma((8,)), dma((8,)), dma((16,)), dma((16,)),
        ],
        compiler_params=pltpu.CompilerParams(
            collective_id=0, has_side_effects=True, vmem_limit_bytes=56 * 1024 * 1024
        ),
    )(pixels, ws, dk, we, wr, wd, wo, tissue, owners, cot)


def solution(mesh):
    placed = (
        P(None, "row", "col"), P(), P(), P(), P(), P(), P("row", "col", None, None),
        P("row", "col"), P("row", "col", None), P("row", "col", None),
    )
    return jax.shard_map(
        on_device,
        mesh=mesh,
        in_specs=placed,
        out_specs=(P(), P(), P(), P(), P(), P("row", "col", None, None)),
        check_vma=False,
    )
```

```python
import jax
import jax.numpy as jnp
from jax import lax
from jax.experimental import pallas as pl
from jax.experimental.pallas import tpu as pltpu
from jax.sharding import PartitionSpec as P

C0, C1, HID, E = 96, 192, 384, 768
ROWS, COLS = 8, 16
BF, F32, I32 = jnp.bfloat16, jnp.float32, jnp.int32
EPS = 1e-06
SLOPE = 0.7978845608028654
CUBIC = 0.044715
MESH = pl.DeviceIdType.MESH
NEAR = ((-1, 0), (1, 0), (0, -1), (0, 1), (-1, -1), (-1, 1), (1, -1), (1, 1))

NN = (((1,), (0,)), ((), ()))
NT = (((1,), (1,)), ((), ()))
TN = (((0,), (0,)), ((), ()))


def dot(a, b, dims=NN):
    return lax.dot_general(a, b, dims, preferred_element_type=F32)


def iota(shape, dim):
    return lax.broadcasted_iota(I32, shape, dim)


def norm_lanes(x, mask):
    mean = jnp.sum(x, axis=-1, keepdims=True) * (1.0 / C0)
    center = (x - mean) * mask
    scale = lax.rsqrt(jnp.sum(center * center, axis=-1, keepdims=True) * (1.0 / C0) + EPS)
    return center * scale, scale


def norm_back_lanes(normed, scale, grad):
    mean = jnp.sum(grad, axis=-1, keepdims=True) * (1.0 / C0)
    proj = jnp.sum(grad * normed, axis=-1, keepdims=True) * (1.0 / C0)
    return scale * (grad - mean - normed * proj)


def gelu_both(h):
    sq = h * h
    t = jnp.tanh(SLOPE * h * (1.0 + CUBIC * sq))
    half = 0.5 * (1.0 + t)
    return h * half, half + 0.5 * h * (1.0 - t * t) * (SLOPE * (1.0 + 3.0 * CUBIC * sq))


def depthwise(src, kb, dst, flip):
    def body(n, carry):
        ib, jb = n // 8, n % 8
        i0 = ib * 8
        acc = [None] * 8
        for v in range(7):
            taps = []
            for u in range(7):
                tap = 7 * u + v
                taps.append(kb[48 - tap if flip else tap])
            for r in range(14):
                x = src[i0 + r + 1, pl.ds(jb * 8 + v, 8), :]
                for u in range(7):
                    i = r - u
                    if 0 <= i < 8:
                        term = taps[u] * x
                        acc[i] = term if acc[i] is None else acc[i] + term
        for i in range(8):
            dst[i0 + i, pl.ds(pl.multiple_of(jb * 8, 8), 8), :] = acc[i]
        return carry

    lax.fori_loop(0, 32, body, 0)


def kernel(
    pix, ws, dkt, we, wrt, wdt, wo, tissue, owners, cot,
    out_stem, out_taps, out_expand, out_reduce, out_down, out_owner,
    xe, perm, permi, wblk, ws128, kb, we128, wr128, dwt,
    pad, sn, ss, ft, conv, mn, ms, mb, act, slope, dn, ds, gp, pmt,
    cots, sbuf, rbuf, rets, ret, nball, pgall, wt, gs, dgu, dgp, hrow, hcol, hcor,
    acc_s, acc_e, acc_r,
    g1, g1r1, g1p2, g1r2, g1p3, g1a, g2, g2r1, g2p2, g2r2, g2p3, g2a, kt, g3a, g3r, g3b, g3c,
    px_s, px_r, a_s, a_r, b_s, b_r, h_s, h_r,
    p1_s, p1_r, p2_s, p2_r, p3_s, p3_r, q1_s, q1_r, q2_s, q2_r, q3_s, q3_r, r1_s, r1_r, r2_s, r2_r,
):
    row, col = lax.axis_index("row"), lax.axis_index("col")

    def near(n):
        dr, dc = NEAR[n]
        return lax.rem(row + (dr + ROWS), ROWS), lax.rem(col + (dc + COLS), COLS)

    def col_peer(k):
        return row, lax.rem(col + k, COLS)

    def row_peer(k):
        return lax.rem(row + k, ROWS), col

    def remote(src, dst, send, recv, dev):
        return pltpu.make_async_remote_copy(
            src_ref=src, dst_ref=dst, send_sem=send, recv_sem=recv, device_id=dev, device_id_type=MESH
        )

    barrier = pltpu.get_barrier_semaphore()
    for k in range(1, COLS):
        pl.semaphore_signal(barrier, inc=1, device_id=col_peer(k), device_id_type=MESH)
    for k in range(1, ROWS):
        pl.semaphore_signal(barrier, inc=1, device_id=row_peer(k), device_id_type=MESH)
    for n in range(4, 8):
        pl.semaphore_signal(barrier, inc=1, device_id=near(n), device_id_type=MESH)
    pl.semaphore_wait(barrier, (COLS - 1) + (ROWS - 1) + 4)

    px_src = (
        pix.at[:, 0:16, :], pix.at[:, 112:128, :], pix.at[:, :, 0:128], pix.at[:, :, 128:256],
        pix.at[:, 0:16, 0:128], pix.at[:, 0:16, 128:256], pix.at[:, 112:128, 0:128], pix.at[:, 112:128, 128:256],
    )
    px_dst = (
        xe.at[:, 144:160, 128:384], xe.at[:, 0:16, 128:384], xe.at[:, 16:144, 384:512], xe.at[:, 16:144, 0:128],
        xe.at[:, 144:160, 384:512], xe.at[:, 144:160, 0:128], xe.at[:, 0:16, 384:512], xe.at[:, 0:16, 0:128],
    )
    px = [remote(px_src[n], px_dst[n], px_s.at[n], px_r.at[n], near(n)) for n in range(8)]
    for n in range(8):
        px[n].start()

    mask = (iota((1, 128), 1) < C0).astype(F32)
    xe[:, 16:144, 128:384] = pix[...]
    pr = iota((288, 512), 0)
    perm[...] = (iota((288, 512), 1) == 116 + 4 * (pr % 72) + pr // 72).astype(F32).astype(BF)
    for s in range(4):
        permi[s] = (iota((256, 64), 0) == 4 * iota((256, 64), 1) + s).astype(F32).astype(BF)
    ws128[...] = jnp.zeros_like(ws128)
    ws128[:, 0:C0] = ws[...]
    q48 = iota((48, 48), 0)
    ql = iota((48, 128), 0)
    for s in range(4):
        pick = (iota((48, 48), 1) == (q48 // 16) * 16 + (q48 % 4) * 4 + s).astype(F32).astype(BF)
        wsel = dot(pick, ws128[...])
        for i4 in range(4):
            wblk[s, :, i4 * 128 : (i4 + 1) * 128] = jnp.where((ql // 4) % 4 == i4, wsel, 0.0).astype(BF)
    kb[...] = jnp.zeros_like(kb)
    for t in range(49):
        kb[t, :, 0:C0] = jnp.broadcast_to(dkt[t : t + 1, :], (8, C0))
    we128[...] = jnp.zeros_like(we128)
    we128[0:C0, :] = we[...]
    wr128[...] = jnp.zeros_like(wr128)
    wr128[0:C0, :] = wrt[...]
    dwt[...] = jnp.zeros_like(dwt)
    for b in range(4):
        dwt[:, b * 128 : b * 128 + C0] = wdt[:, b * C0 : (b + 1) * C0]
    wt[...] = wo[0, 0].astype(F32).T.astype(BF)

    slots = []
    for p in range(8):
        rank = 0
        for q in range(p):
            same = jnp.where(owners[0, q] == owners[0, p], 1, 0)
            rank = rank + same * tissue[q // 4, q % 4]
        slots.append(jnp.where(tissue[p // 4, p % 4] == 1, owners[0, p] * 2 + rank, -1000))
    rr = iota((512, 128), 0)
    ll = iota((512, 128), 1)
    patch = (rr // 256) * 4 + (rr % 32) // 8
    slot_row = jnp.zeros((512, 128), I32)
    for p in range(8):
        slot_row = jnp.where(patch == p, slots[p], slot_row)
    hit = jnp.where(((rr // 32) % 8) * 8 + rr % 8 == ll % 64, slot_row - ll // 64, -2000)
    for d in range(COLS):
        pmt[:, d * 128 : (d + 1) * 128] = (hit == 2 * d).astype(F32).astype(BF)
    cots[...] = jnp.zeros_like(cots)
    cots[0:4, :] = cot[0].astype(F32)
    cots[4:8, :] = cot[1].astype(F32)
    slot_lane = jnp.full((256, 16), -1000, I32)
    for p in range(8):
        slot_lane = jnp.where(iota((256, 16), 1) == p, slots[p], slot_lane)
    ro = iota((256, 16), 0)
    rem16 = ro % 16
    want = jnp.where(rem16 < 12, 2 * (ro // 16) + rem16 // 6, -3000)
    packed = jnp.zeros((256, 128), F32)
    for b in range(6):
        choose = jnp.where(rem16 % 6 == b, want, -3000)
        packed = packed + dot(
            (slot_lane == choose).astype(F32).astype(BF), cots[:, b * 128 : (b + 1) * 128].astype(BF)
        )
    for d in range(COLS):
        sbuf[d, C1 : C1 + 16, :] = packed[d * 16 : (d + 1) * 16].astype(BF)

    for n in range(8):
        px[n].wait_recv()

    @pl.when(row == 0)
    def _():
        xe[:, 0:16, :] = jnp.zeros((3, 16, 512), BF)

    @pl.when(row == ROWS - 1)
    def _():
        xe[:, 144:160, :] = jnp.zeros((3, 16, 512), BF)

    @pl.when(col == 0)
    def _():
        xe[:, :, 0:128] = jnp.zeros((3, 160, 128), BF)

    @pl.when(col == COLS - 1)
    def _():
        xe[:, :, 384:512] = jnp.zeros((3, 160, 128), BF)

    def stem_body(g, carry):
        at = pl.ds(pl.multiple_of(g * 16, 16), 16)
        xg = jnp.concatenate([xe[0, at, :], xe[1, at, :], xe[2, at, :]], axis=0)
        turned = dot(perm[...], xg, NT)
        total = jnp.zeros((72, 512), F32)
        for s in range(4):
            total = total + dot(turned[s * 72 : (s + 1) * 72].astype(BF), wblk[s])
        for i4 in range(4):
            normed, scale = norm_lanes(total[:, i4 * 128 : (i4 + 1) * 128], mask)
            pad[4 * g + i4] = normed.astype(BF).astype(F32)
            sn[4 * g + i4] = normed
            ss[4 * g + i4] = jnp.broadcast_to(scale, (72, 128))
        return carry

    lax.fori_loop(0, 10, stem_body, 0, unroll=10)

    def flat_body(g, carry):
        at = pl.ds(pl.multiple_of(g * 16 + 16, 16), 16)
        xg = jnp.concatenate([xe[0, at, 128:384], xe[1, at, 128:384], xe[2, at, 128:384]], axis=0)
        for s in range(4):
            ft[g, s * 48 : (s + 1) * 48, :] = dot(xg, permi[s]).astype(BF)
        return carry

    lax.fori_loop(0, 8, flat_body, 0, unroll=8)

    depthwise(pad, kb, conv, False)

    def mlp_body(b, carry):
        rows4 = pl.ds(b * 4, 4)
        rows = pl.ds(pl.multiple_of(b * 256, 256), 256)
        normed, scale = norm_lanes(conv[rows4].reshape(256, 128), mask)
        mn[rows, :] = normed
        ms[rows, :] = jnp.broadcast_to(scale, (256, 128))
        mixed = normed.astype(BF)
        mb[rows, :] = mixed
        value, grad = gelu_both(dot(mixed, we128[...]))
        value = value.astype(BF)
        act[rows, :] = value
        slope[rows, :] = grad.astype(BF)
        block = jnp.concatenate([pad[b * 4 + 4 + i, 3:67, :] for i in range(4)], axis=0)
        block = block + dot(value, wr128[...], NT)
        normed, scale = norm_lanes(block, mask)
        dn[rows4] = normed.reshape(4, 64, 128)
        ds[rows, :] = jnp.broadcast_to(scale, (256, 128))
        return carry

    lax.fori_loop(0, 8, mlp_body, 0, unroll=8)

    def group_body(i, carry):
        rows = pl.ds(pl.multiple_of(i * 32, 32), 32)
        for u in range(2):
            for v in range(2):
                b = 2 * u + v
                gp[rows, b * 128 : (b + 1) * 128] = dn[2 * i + u, pl.ds(v, 32, stride=2), :].astype(BF)
        return carry

    lax.fori_loop(0, 16, group_body, 0)
    embed = dot(dwt[...], gp[...], NT).astype(BF)

    for d in range(COLS):
        sbuf[d, 0:C1, :] = dot(embed, pmt[:, d * 128 : (d + 1) * 128]).astype(BF)
    def out_copy(k):
        peer = col_peer(k)
        lanes = slice((k % 2) * 128, (k % 2 + 1) * 128)
        return remote(sbuf.at[peer[1]], rbuf.at[k // 2, :, lanes], a_s.at[k], a_r.at[k], peer)

    for k in range(1, COLS):
        out_copy(k).start()
    rbuf[0, :, 0:128] = sbuf[col]

    sel = (iota((16, E), 0) == ((iota((16, E), 1) % 128) // 64) * 6 + iota((16, E), 1) // 128).astype(F32).astype(BF)
    cot_scale = (ROWS * COLS) ** (-0.5) / 8.0
    mine = pl.ds(pl.multiple_of(col * 128, 128), 128)

    def back_copy(j, half):
        k = 2 * j + half
        dev = (row, lax.rem(col - k + COLS, COLS))
        lanes = slice(half * 128, (half + 1) * 128)
        return remote(rets.at[j, :, lanes], ret.at[:, mine], b_s.at[k], b_r.at[k], dev)

    def own(j):
        cells = rbuf[j, 0:C1, :].astype(F32)
        mean = jnp.sum(cells, axis=0, keepdims=True) * (1.0 / C1)
        center = cells - mean
        scale = lax.rsqrt(jnp.sum(center * center, axis=0, keepdims=True) * (1.0 / C1) + EPS)
        normed = center * scale
        nb = normed.astype(BF)
        nball[j] = nb
        cots_a = dot(rbuf[j, C1 : C1 + 16, 0:128], sel, TN) * cot_scale
        cots_b = dot(rbuf[j, C1 : C1 + 16, 128:256], sel, TN) * cot_scale
        for b in range(6):
            lanes = slice(b * 128, (b + 1) * 128)
            pre = dot(wt[lanes, :], nb)
            cott = jnp.concatenate([cots_a[:, lanes], cots_b[:, lanes]], axis=1)
            pgall[j, lanes, :] = (cott * gelu_both(pre)[1]).astype(BF)
        back = dot(wo[0, 0], pgall[j])
        mean = jnp.sum(back, axis=0, keepdims=True) * (1.0 / C1)
        proj = jnp.sum(back * normed, axis=0, keepdims=True) * (1.0 / C1)
        rets[j] = (scale * (back - mean - normed * proj)).astype(BF)

    out_copy(1).wait_recv()
    own(0)
    ret[:, mine] = rets[0, :, 0:128]
    back_copy(0, 1).start()

    def own_body(j, carry):
        for half in range(2):
            k = 2 * j + half
            lanes = slice(half * 128, (half + 1) * 128)
            remote(sbuf.at[0], rbuf.at[j, :, lanes], a_s.at[k], a_r.at[k], col_peer(k)).wait_recv()
        own(j)
        for half in range(2):
            back_copy(j, half).start()
        return carry

    lax.fori_loop(1, COLS // 2, own_body, 0)
    for k in range(1, COLS):
        out_copy(k).wait_send()
    for k in range(1, COLS):
        back_copy(k // 2, k % 2).wait_recv()
    eg = dot(ret[...], pmt[...], NT).astype(BF)
    egt = dot(pmt[...], ret[...], NT).astype(BF)

    def make_sum(g, r1, p2, r2, p3, ga, s1, t1, s2, t2, s3, t3):
        first = [
            remote(g.at[col_peer(k)[1]], r1.at[k], s1.at[k], t1.at[k], col_peer(k)) for k in range(1, COLS)
        ]
        second = [remote(p2, r2.at[row], s2.at[k], t2.at[k], row_peer(k)) for k in range(1, ROWS)]
        third = [remote(p3, ga.at[col], s3.at[k], t3.at[k], col_peer(k)) for k in range(1, COLS)]

        def start():
            for cp in first:
                cp.start()

        def turn():
            for cp in first:
                cp.wait_recv()
            total = g[col].astype(F32)
            for k in range(1, COLS):
                total = total + r1[k].astype(F32)
            p2[...] = total.astype(p2.dtype)
            r2[row] = total.astype(p2.dtype)
            for cp in second:
                cp.start()

        def spread():
            for cp in second:
                cp.wait_recv()
            total = r2[0].astype(F32)
            for k in range(1, ROWS):
                total = total + r2[k].astype(F32)
            p3[...] = total.astype(p3.dtype)
            ga[col] = total.astype(p3.dtype)
            for cp in third:
                cp.start()

        def finish():
            for cp in third:
                cp.wait_recv()

        def drain():
            for cp in first + second + third:
                cp.wait_send()

        return start, turn, spread, finish, drain

    start1, turn1, spread1, finish1, drain1 = make_sum(
        g1, g1r1, g1p2, g1r2, g1p3, g1a, p1_s, p1_r, p2_s, p2_r, p3_s, p3_r
    )
    start2, turn2, spread2, finish2, drain2 = make_sum(
        g2, g2r1, g2p2, g2r2, g2p3, g2a, q1_s, q1_r, q2_s, q2_r, q3_s, q3_r
    )
    stem_rows = [remote(g3a, g3r.at[row], r1_s.at[k], r1_r.at[k], row_peer(k)) for k in range(1, ROWS)]
    stem_cols = [remote(g3b, g3c.at[col], r2_s.at[k], r2_r.at[k], col_peer(k)) for k in range(1, COLS)]

    for b in range(4):
        lanes = slice(b * 128, (b + 1) * 128)
        part = dot(eg, gp[:, lanes]).astype(BF)
        for n in range(4):
            g1[4 * b + n] = part[n * 48 : (n + 1) * 48]
    start1()

    gb = dot(egt, dwt[...])
    for i in range(16):
        for b in range(4):
            gs[2 * i + b // 2, pl.ds(b % 2, 32, stride=2), :] = gb[i * 32 : (i + 1) * 32, b * 128 : (b + 1) * 128]

    acc_e[...] = jnp.zeros_like(acc_e)
    acc_r[...] = jnp.zeros_like(acc_r)

    def back_body(b, carry):
        rows4 = pl.ds(b * 4, 4)
        rows = pl.ds(pl.multiple_of(b * 256, 256), 256)
        grad = gs[rows4].reshape(256, 128)
        grad = norm_back_lanes(dn[rows4].reshape(256, 128), ds[rows, :], grad) * mask
        gs[rows4] = grad.reshape(4, 64, 128)
        og = grad.astype(BF)
        acc_r[...] += dot(og, act[rows, :], TN)
        hid = (dot(og, wr128[...]) * slope[rows, :].astype(F32)).astype(BF)
        acc_e[...] += dot(mb[rows, :], hid, TN)
        mg = dot(hid, we128[...], NT)
        dg = norm_back_lanes(mn[rows, :], ms[rows, :], mg) * mask
        dgu[rows4] = dg.reshape(4, 64, 128)
        return carry

    lax.fori_loop(0, 8, back_body, 0, unroll=4)

    h_src = (
        dgu.at[0:3], dgu.at[29:32], dgu.at[:, 0:8, :], dgu.at[:, 56:64, :],
        dgu.at[0:3, 0:8, :], dgu.at[0:3, 56:64, :], dgu.at[29:32, 0:8, :], dgu.at[29:32, 56:64, :],
    )
    h_dst = (
        hrow.at[1], hrow.at[0], hcol.at[1], hcol.at[0], hcor.at[3], hcor.at[2], hcor.at[1], hcor.at[0],
    )
    halo = [remote(h_src[n], h_dst[n], h_s.at[n], h_r.at[n], near(n)) for n in range(8)]
    for n in range(8):
        halo[n].start()

    turn1()
    for b in range(3):
        lanes = slice(b * 128, (b + 1) * 128)
        for n in range(2):
            g2[2 * b + n] = acc_e[n * 48 : (n + 1) * 48, lanes].astype(BF)
            g2[6 + 2 * b + n] = acc_r[n * 48 : (n + 1) * 48, lanes].astype(BF)

    kt[...] = jnp.zeros_like(kt)
    for v in range(7):

        def taps_body(jb, acc, v=v):
            acc = list(acc)
            here = pl.ds(pl.multiple_of(jb * 8, 8), 8)
            grads = {}
            for r in range(38):
                x = pad[r + 1, pl.ds(jb * 8 + v, 8), :]
                if r < 32:
                    grads[r] = dgu[r, here, :]
                for u in range(7):
                    if 0 <= r - u < 32:
                        acc[u] = acc[u] + grads[r - u] * x
            return tuple(acc)

        sums = lax.fori_loop(0, 8, taps_body, tuple(jnp.zeros((8, 128), F32) for _ in range(7)))
        for u in range(7):
            kt[7 * u + v : 7 * u + v + 1, :] = jnp.sum(sums[u], axis=0, keepdims=True)
    g2[12] = kt[0:48].astype(BF)
    g2[13] = kt[48:96].astype(BF)
    g2[14] = jnp.zeros((48, 128), BF)
    g2[15] = jnp.zeros((48, 128), BF)
    start2()
    spread1()

    dgp[...] = jnp.zeros_like(dgp)
    for i in range(32):
        dgp[4 + i, 3:67, :] = dgu[i]
    for n in range(8):
        halo[n].wait_recv()
    top, bottom = jnp.where(row > 0, 1.0, 0.0), jnp.where(row < ROWS - 1, 1.0, 0.0)
    left, right = jnp.where(col > 0, 1.0, 0.0), jnp.where(col < COLS - 1, 1.0, 0.0)
    for i in range(3):
        dgp[1 + i, 3:67, :] = hrow[0, i] * top
        dgp[36 + i, 3:67, :] = hrow[1, i] * bottom
        dgp[1 + i, 0:3, :] = hcor[0, i, 5:8] * (top * left)
        dgp[1 + i, 67:70, :] = hcor[1, i, 0:3] * (top * right)
        dgp[36 + i, 0:3, :] = hcor[2, i, 5:8] * (bottom * left)
        dgp[36 + i, 67:70, :] = hcor[3, i, 0:3] * (bottom * right)
    dgp[4:36, 0:3, :] = hcol[0, :, 5:8, :] * left
    dgp[4:36, 67:70, :] = hcol[1, :, 0:3, :] * right

    depthwise(dgp, kb, conv, True)
    turn2()

    acc_s[...] = jnp.zeros_like(acc_s)

    def stem_back(g, carry):
        parts = []
        for i in range(4):
            grad = gs[4 * g + i] + conv[4 * g + i]
            parts.append(
                norm_back_lanes(sn[4 * g + 4 + i, 3:67, :], ss[4 * g + 4 + i, 3:67, :], grad).astype(BF)
            )
        grads = jnp.concatenate(parts, axis=1)
        for s in range(4):
            acc_s[s * 48 : (s + 1) * 48, :] += dot(ft[g, s * 48 : (s + 1) * 48, :], grads)
        return carry

    lax.fori_loop(0, 8, stem_back, 0, unroll=4)
    rows = iota((192, 128), 0)
    folded = jnp.zeros((192, 128), F32)
    for i4 in range(4):
        folded = folded + jnp.where((rows // 4) % 4 == i4, acc_s[:, i4 * 128 : (i4 + 1) * 128], 0.0)
    m48, q192 = iota((48, 192), 0), iota((48, 192), 1)
    rem = q192 % 48
    gather = (m48 == (rem // 16) * 16 + (rem % 4) * 4 + q192 // 48).astype(F32)
    stem = lax.dot_general(gather, folded, NN, precision=lax.Precision.HIGHEST, preferred_element_type=F32)
    g3a[...] = stem.astype(BF)
    g3r[row] = stem.astype(BF)
    for cp in stem_rows:
        cp.start()
    finish1()
    for b in range(4):
        for n in range(4):
            out_down[n * 48 : (n + 1) * 48, b * C0 : (b + 1) * C0] = g1a[4 * b + n, :, 0:C0].astype(F32)
    spread2()
    for cp in stem_rows:
        cp.wait_recv()
    total = g3r[0].astype(F32)
    for k in range(1, ROWS):
        total = total + g3r[k].astype(F32)
    g3b[...] = total.astype(BF)
    g3c[col] = total.astype(BF)
    for cp in stem_cols:
        cp.start()

    for b in range(6):
        lanes = slice(b * 128, (b + 1) * 128)
        part = dot(nball[0], pgall[0, lanes, :], NT)
        for j in range(1, COLS // 2):
            part = part + dot(nball[j], pgall[j, lanes, :], NT)
        out_owner[0, 0, :, lanes] = part

    finish2()
    for b in range(3):
        lanes = slice(b * 128, (b + 1) * 128)
        for n in range(2):
            at = slice(n * 48, (n + 1) * 48)
            out_expand[at, lanes] = g2a[2 * b + n].astype(F32)
            out_reduce[at, lanes] = g2a[6 + 2 * b + n].astype(F32)
    out_taps[0:48, :] = g2a[12].astype(F32)[:, 0:C0]
    out_taps[48:49, :] = g2a[13].astype(F32)[0:1, 0:C0]
    for cp in stem_cols:
        cp.wait_recv()
    total = g3c[0].astype(F32)
    for k in range(1, COLS):
        total = total + g3c[k].astype(F32)
    out_stem[...] = total[:, 0:C0]

    for n in range(8):
        px[n].wait_send()
        halo[n].wait_send()
    for k in range(1, COLS):
        back_copy(k // 2, k % 2).wait_send()
    drain1()
    drain2()
    for cp in stem_rows + stem_cols:
        cp.wait_send()


def on_device(pixels, ws, dk, we, wr, wd, wo, tissue, owners, cot):
    vmem = pl.BlockSpec(memory_space=pltpu.VMEM)
    smem = pl.BlockSpec(memory_space=pltpu.SMEM)
    dma = pltpu.SemaphoreType.DMA
    V = pltpu.VMEM
    outs = ((48, C0), (49, C0), (C0, HID), (C0, HID), (C1, 4 * C0), (1, 1, C1, E))
    stem, taps, expand, reduce, down, owner = pl.pallas_call(
        kernel,
        out_shape=tuple(jax.ShapeDtypeStruct(s, F32) for s in outs),
        in_specs=[vmem] * 7 + [smem, smem, vmem],
        out_specs=(vmem,) * 6,
        scratch_shapes=[
            V((3, 160, 512), BF), V((288, 512), BF), V((4, 256, 64), BF), V((4, 48, 512), BF), V((48, 128), BF),
            V((49, 8, 128), F32), V((128, HID), BF), V((128, HID), BF), V((C1, 512), BF),
            V((40, 72, 128), F32), V((40, 72, 128), F32), V((40, 72, 128), F32), V((8, 192, 64), BF),
            V((32, 64, 128), F32), V((2048, 128), F32), V((2048, 128), F32), V((2048, 128), BF),
            V((2048, HID), BF), V((2048, HID), BF), V((32, 64, 128), F32), V((2048, 128), F32),
            V((512, 512), BF), V((512, 2048), BF),
            V((16, E), F32), V((16, 208, 128), BF), V((8, 208, 256), BF), V((8, C1, 256), BF), V((C1, 2048), BF),
            V((8, C1, 256), BF), V((8, E, 256), BF),
            V((E, C1), BF), V((32, 64, 128), F32), V((32, 64, 128), F32), V((40, 72, 128), F32),
            V((2, 3, 64, 128), F32), V((2, 32, 8, 128), F32), V((4, 3, 8, 128), F32),
            V((192, 512), F32), V((128, HID), F32), V((128, HID), F32),
            V((16, 48, 128), BF), V((16, 48, 128), BF), V((48, 128), BF), V((8, 48, 128), BF), V((48, 128), BF),
            V((16, 48, 128), BF),
            V((16, 48, 128), BF), V((16, 48, 128), BF), V((48, 128), BF), V((8, 48, 128), BF), V((48, 128), BF),
            V((16, 48, 128), BF),
            V((96, 128), F32), V((48, 128), BF), V((8, 48, 128), BF), V((48, 128), BF), V((16, 48, 128), BF),
            dma((8,)), dma((8,)), dma((16,)), dma((16,)), dma((16,)), dma((16,)), dma((8,)), dma((8,)),
            dma((16,)), dma((16,)), dma((8,)), dma((8,)), dma((16,)), dma((16,)),
            dma((16,)), dma((16,)), dma((8,)), dma((8,)), dma((16,)), dma((16,)), dma((8,)), dma((8,)), dma((16,)), dma((16,)),
        ],
        compiler_params=pltpu.CompilerParams(
            collective_id=0, has_side_effects=True, vmem_limit_bytes=56 * 1024 * 1024
        ),
    )(pixels, ws, dk.T, we, wr.T, wd.T, wo, tissue, owners.reshape(1, 8), cot)
    return stem, taps.T, expand, reduce.T, down.T, owner


def solution(mesh):
    placed = (
        P(None, "row", "col"), P(), P(), P(), P(), P(), P("row", "col", None, None),
        P("row", "col"), P("row", "col", None), P("row", "col", None),
    )
    return jax.shard_map(
        on_device,
        mesh=mesh,
        in_specs=placed,
        out_specs=(P(), P(), P(), P(), P(), P("row", "col", None, None)),
        check_vma=False,
    )
```

```python
import jax
import jax.numpy as jnp
from jax import lax
from jax.experimental import pallas as pl
from jax.experimental.pallas import tpu as pltpu
from jax.sharding import PartitionSpec as P

C0, C1, HID, E = 96, 192, 384, 768
ROWS, COLS = 8, 16
BF, F32, I32 = jnp.bfloat16, jnp.float32, jnp.int32
EPS = 1e-06
SLOPE = 0.7978845608028654
CUBIC = 0.044715
MESH = pl.DeviceIdType.MESH
NEAR = ((-1, 0), (1, 0), (0, -1), (0, 1), (-1, -1), (-1, 1), (1, -1), (1, 1))

NN = (((1,), (0,)), ((), ()))
NT = (((1,), (1,)), ((), ()))
TN = (((0,), (0,)), ((), ()))


def dot(a, b, dims=NN):
    return lax.dot_general(a, b, dims, preferred_element_type=F32)


def iota(shape, dim):
    return lax.broadcasted_iota(I32, shape, dim)


def norm_lanes(x, mask):
    mean = jnp.sum(x, axis=-1, keepdims=True) * (1.0 / C0)
    center = (x - mean) * mask
    scale = lax.rsqrt(jnp.sum(center * center, axis=-1, keepdims=True) * (1.0 / C0) + EPS)
    return center * scale, scale


def norm_back_lanes(normed, scale, grad):
    mean = jnp.sum(grad, axis=-1, keepdims=True) * (1.0 / C0)
    proj = jnp.sum(grad * normed, axis=-1, keepdims=True) * (1.0 / C0)
    return scale * (grad - mean - normed * proj)


def gelu_both(h):
    sq = h * h
    t = jnp.tanh(SLOPE * h * (1.0 + CUBIC * sq))
    half = 0.5 * (1.0 + t)
    return h * half, half + 0.5 * h * (1.0 - t * t) * (SLOPE * (1.0 + 3.0 * CUBIC * sq))


def depthwise(src, kb, dst, flip, count=32, tile=lambda n: (n // 8, n % 8)):
    def body(n, carry):
        ib, jb = tile(n)
        i0 = ib * 8
        acc = [None] * 8
        for v in range(7):
            taps = []
            for u in range(7):
                tap = 7 * u + v
                taps.append(kb[48 - tap if flip else tap])
            for r in range(14):
                x = src[i0 + r + 1, pl.ds(jb * 8 + v, 8), :]
                for u in range(7):
                    i = r - u
                    if 0 <= i < 8:
                        term = taps[u] * x
                        acc[i] = term if acc[i] is None else acc[i] + term
        for i in range(8):
            dst[i0 + i, pl.ds(pl.multiple_of(jb * 8, 8), 8), :] = acc[i]
        return carry

    lax.fori_loop(0, count, body, 0, unroll=2)


def kernel(
    pix, ws, dkt, we, wrt, wdt, wo, tissue, owners, cot,
    out_stem, out_taps, out_expand, out_reduce, out_down, out_owner,
    xe, perm, perms, permi, wblk, ws128, kb, we128, wr128, dwt,
    pad, sn, ss, ft, conv, mn, ms, mb, act, slope, dn, ds, gp, pmt,
    cots, sbuf, rbuf, rets, ret, nball, pgall, wt, gs, dgu, dgp, hrow, hcol, hcor,
    acc_s, acc_e, acc_r,
    g1, g1r1, g1p2, g1r2, g1p3, g1a, g2, g2r1, g2p2, g2r2, g2p3, g2a, kt, g3s, g3t, g3a, g3r, g3b, g3c, g4a, g4r, g4b, g4c,
    px_s, px_r, a_s, a_r, b_s, b_r, h_s, h_r,
    p1_s, p1_r, p2_s, p2_r, p3_s, p3_r, q1_s, q1_r, q2_s, q2_r, q3_s, q3_r, r1_s, r1_r, r2_s, r2_r,
    r0_s, r0_r, t1_s, t1_r, t2_s, t2_r,
):
    row, col = lax.axis_index("row"), lax.axis_index("col")

    def near(n):
        dr, dc = NEAR[n]
        return lax.rem(row + (dr + ROWS), ROWS), lax.rem(col + (dc + COLS), COLS)

    def col_peer(k):
        return row, lax.rem(col + k, COLS)

    def row_peer(k):
        return lax.rem(row + k, ROWS), col

    def remote(src, dst, send, recv, dev):
        return pltpu.make_async_remote_copy(
            src_ref=src, dst_ref=dst, send_sem=send, recv_sem=recv, device_id=dev, device_id_type=MESH
        )

    barrier = pltpu.get_barrier_semaphore()
    for k in range(1, COLS):
        pl.semaphore_signal(barrier, inc=1, device_id=col_peer(k), device_id_type=MESH)
    for k in range(1, ROWS):
        pl.semaphore_signal(barrier, inc=1, device_id=row_peer(k), device_id_type=MESH)
    for n in range(4, 8):
        pl.semaphore_signal(barrier, inc=1, device_id=near(n), device_id_type=MESH)
    pl.semaphore_wait(barrier, (COLS - 1) + (ROWS - 1) + 4)

    px_src = (
        pix.at[:, 0:16, :], pix.at[:, 112:128, :], pix.at[:, :, 0:128], pix.at[:, :, 128:256],
        pix.at[:, 0:16, 0:128], pix.at[:, 0:16, 128:256], pix.at[:, 112:128, 0:128], pix.at[:, 112:128, 128:256],
    )
    px_dst = (
        xe.at[:, 144:160, 128:384], xe.at[:, 0:16, 128:384], xe.at[:, 16:144, 384:512], xe.at[:, 16:144, 0:128],
        xe.at[:, 144:160, 384:512], xe.at[:, 144:160, 0:128], xe.at[:, 0:16, 384:512], xe.at[:, 0:16, 0:128],
    )
    px = [remote(px_src[n], px_dst[n], px_s.at[n], px_r.at[n], near(n)) for n in range(8)]
    for n in range(8):
        px[n].start()

    mask = (iota((1, 128), 1) < C0).astype(F32)
    pr = iota((256, 256), 0)
    perm[...] = (iota((256, 256), 1) == 4 * (pr % 64) + pr // 64).astype(F32).astype(BF)
    pr = iota((32, 128), 0)
    pl_ = iota((32, 128), 1)
    perms[0] = jnp.where(pr % 8 < 3, (pl_ == 116 + 4 * (pr % 8) + pr // 8).astype(F32), 0.0).astype(BF)
    perms[1] = jnp.where(pr % 8 < 3, (pl_ == 4 * (pr % 8) + pr // 8).astype(F32), 0.0).astype(BF)
    for s in range(4):
        permi[s] = (iota((256, 64), 0) == 4 * iota((256, 64), 1) + s).astype(F32).astype(BF)
    ws128[...] = jnp.zeros_like(ws128)
    ws128[:, 0:C0] = ws[...]
    q48 = iota((48, 48), 0)
    ql = iota((48, 128), 0)
    for s in range(4):
        pick = (iota((48, 48), 1) == (q48 // 16) * 16 + (q48 % 4) * 4 + s).astype(F32).astype(BF)
        wsel = dot(pick, ws128[...])
        for i4 in range(4):
            wblk[s, :, i4 * 128 : (i4 + 1) * 128] = jnp.where((ql // 4) % 4 == i4, wsel, 0.0).astype(BF)
    kb[...] = jnp.zeros_like(kb)
    for t in range(49):
        kb[t, :, 0:C0] = jnp.broadcast_to(dkt[t : t + 1, :], (8, C0))
    we128[...] = jnp.zeros_like(we128)
    we128[0:C0, :] = we[...]
    wr128[...] = jnp.zeros_like(wr128)
    wr128[0:C0, :] = wrt[...]
    dwt[...] = jnp.zeros_like(dwt)
    for b in range(4):
        dwt[:, b * 128 : b * 128 + C0] = wdt[:, b * C0 : (b + 1) * C0]

    def stem_piece(ref, r0, lanes, chooser, width, use):
        at = pl.ds(pl.multiple_of(r0, 16), 16)
        xg = jnp.concatenate([ref[0, at, lanes], ref[1, at, lanes], ref[2, at, lanes]], axis=0)
        turned = dot(chooser, xg, NT)
        total = jnp.zeros((width, 512), F32)
        for s in range(4):
            total = total + dot(turned[s * width : (s + 1) * width].astype(BF), wblk[s])
        for i4 in range(4):
            use(i4, *norm_lanes(total[:, i4 * 128 : (i4 + 1) * 128], mask))

    def stem_body(g, carry):
        def use(i4, normed, scale):
            pad[4 * g + 4 + i4, 3:67, :] = normed.astype(BF).astype(F32)
            sn[4 * g + i4] = normed
            ss[4 * g + i4] = jnp.broadcast_to(scale, (64, 128))

        stem_piece(pix, g * 16, slice(0, 256), perm[...], 64, use)
        return carry

    lax.fori_loop(0, 8, stem_body, 0, unroll=8)

    slots = []
    for p in range(8):
        rank = 0
        for q in range(p):
            same = jnp.where(owners[0, q] == owners[0, p], 1, 0)
            rank = rank + same * tissue[q // 4, q % 4]
        slots.append(jnp.where(tissue[p // 4, p % 4] == 1, owners[0, p] * 2 + rank, -1000))
    rr = iota((512, 128), 0)
    ll = iota((512, 128), 1)
    patch = (rr // 256) * 4 + (rr % 32) // 8
    slot_row = jnp.zeros((512, 128), I32)
    for p in range(8):
        slot_row = jnp.where(patch == p, slots[p], slot_row)
    hit = jnp.where(((rr // 32) % 8) * 8 + rr % 8 == ll % 64, slot_row - ll // 64, -2000)
    for d in range(COLS):
        pmt[:, d * 128 : (d + 1) * 128] = (hit == 2 * d).astype(F32).astype(BF)
    cots[...] = jnp.zeros_like(cots)
    cots[0:4, :] = cot[0].astype(F32)
    cots[4:8, :] = cot[1].astype(F32)
    slot_lane = jnp.full((256, 16), -1000, I32)
    for p in range(8):
        slot_lane = jnp.where(iota((256, 16), 1) == p, slots[p], slot_lane)
    ro = iota((256, 16), 0)
    rem16 = ro % 16
    want = jnp.where(rem16 < 12, 2 * (ro // 16) + rem16 // 6, -3000)
    packed = jnp.zeros((256, 128), F32)
    for b in range(6):
        choose = jnp.where(rem16 % 6 == b, want, -3000)
        packed = packed + dot(
            (slot_lane == choose).astype(F32).astype(BF), cots[:, b * 128 : (b + 1) * 128].astype(BF)
        )
    for d in range(COLS):
        sbuf[d, C1 : C1 + 16, :] = packed[d * 16 : (d + 1) * 16].astype(BF)

    for n in range(8):
        px[n].wait_recv()

    @pl.when(row == 0)
    def _():
        xe[:, 0:16, :] = jnp.zeros((3, 16, 512), BF)

    @pl.when(row == ROWS - 1)
    def _():
        xe[:, 144:160, :] = jnp.zeros((3, 16, 512), BF)

    @pl.when(col == 0)
    def _():
        xe[:, :, 0:128] = jnp.zeros((3, 160, 128), BF)

    @pl.when(col == COLS - 1)
    def _():
        xe[:, :, 384:512] = jnp.zeros((3, 160, 128), BF)

    def side_body(g, carry):
        for side in range(2):
            def use(i4, normed, scale, side=side):
                pad[4 * g + i4, side * 67 : side * 67 + 3, :] = normed[0:3].astype(BF).astype(F32)

            stem_piece(xe, g * 16, slice(side * 384, side * 384 + 128), perms[side], 8, use)
        return carry

    lax.fori_loop(0, 10, side_body, 0, unroll=10)
    for g in (0, 9):

        def use(i4, normed, scale, g=g):
            pad[4 * g + i4, 3:67, :] = normed.astype(BF).astype(F32)

        stem_piece(xe, g * 16, slice(128, 384), perm[...], 64, use)

    depthwise(pad, kb, conv, False)

    def mlp_body(b, carry):
        rows4 = pl.ds(b * 4, 4)
        rows = pl.ds(pl.multiple_of(b * 256, 256), 256)
        normed, scale = norm_lanes(conv[rows4].reshape(256, 128), mask)
        mn[rows, :] = normed
        ms[rows, :] = jnp.broadcast_to(scale, (256, 128))
        mixed = normed.astype(BF)
        mb[rows, :] = mixed
        value, grad = gelu_both(dot(mixed, we128[...]))
        value = value.astype(BF)
        act[rows, :] = value
        slope[rows, :] = grad.astype(BF)
        block = jnp.concatenate([pad[b * 4 + 4 + i, 3:67, :] for i in range(4)], axis=0)
        block = block + dot(value, wr128[...], NT)
        normed, scale = norm_lanes(block, mask)
        dn[rows4] = normed.reshape(4, 64, 128)
        ds[rows, :] = jnp.broadcast_to(scale, (256, 128))
        return carry

    lax.fori_loop(0, 8, mlp_body, 0, unroll=8)

    def group_body(i, carry):
        rows = pl.ds(pl.multiple_of(i * 32, 32), 32)
        for u in range(2):
            for v in range(2):
                b = 2 * u + v
                gp[rows, b * 128 : (b + 1) * 128] = dn[2 * i + u, pl.ds(v, 32, stride=2), :].astype(BF)
        return carry

    lax.fori_loop(0, 16, group_body, 0)
    embed = dot(dwt[...], gp[...], NT).astype(BF)

    for d in range(COLS):
        sbuf[d, 0:C1, :] = dot(embed, pmt[:, d * 128 : (d + 1) * 128]).astype(BF)
    def out_copy(k):
        peer = col_peer(k)
        lanes = slice((k % 2) * 128, (k % 2 + 1) * 128)
        return remote(sbuf.at[peer[1]], rbuf.at[k // 2, :, lanes], a_s.at[k], a_r.at[k], peer)

    for k in range(1, COLS):
        out_copy(k).start()
    rbuf[0, :, 0:128] = sbuf[col]

    sel = (iota((16, E), 0) == ((iota((16, E), 1) % 128) // 64) * 6 + iota((16, E), 1) // 128).astype(F32).astype(BF)
    cot_scale = (ROWS * COLS) ** (-0.5) / 8.0
    mine = pl.ds(pl.multiple_of(col * 128, 128), 128)

    def back_copy(j, half):
        k = 2 * j + half
        dev = (row, lax.rem(col - k + COLS, COLS))
        lanes = slice(half * 128, (half + 1) * 128)
        return remote(rets.at[j, :, lanes], ret.at[:, mine], b_s.at[k], b_r.at[k], dev)

    def own(j):
        cells = rbuf[j, 0:C1, :].astype(F32)
        mean = jnp.sum(cells, axis=0, keepdims=True) * (1.0 / C1)
        center = cells - mean
        scale = lax.rsqrt(jnp.sum(center * center, axis=0, keepdims=True) * (1.0 / C1) + EPS)
        normed = center * scale
        nb = normed.astype(BF)
        nball[j] = nb
        cots_a = dot(rbuf[j, C1 : C1 + 16, 0:128], sel, TN) * cot_scale
        cots_b = dot(rbuf[j, C1 : C1 + 16, 128:256], sel, TN) * cot_scale
        for b in range(6):
            lanes = slice(b * 128, (b + 1) * 128)
            pre = dot(wt[lanes, :], nb)
            cott = jnp.concatenate([cots_a[:, lanes], cots_b[:, lanes]], axis=1)
            pgall[j, lanes, :] = (cott * gelu_both(pre)[1]).astype(BF)
        back = dot(wo[0, 0], pgall[j])
        mean = jnp.sum(back, axis=0, keepdims=True) * (1.0 / C1)
        proj = jnp.sum(back * normed, axis=0, keepdims=True) * (1.0 / C1)
        rets[j] = (scale * (back - mean - normed * proj)).astype(BF)

    wt[...] = wo[0, 0].astype(F32).T.astype(BF)
    def flat_body(g, carry):
        at = pl.ds(pl.multiple_of(g * 16, 16), 16)
        xg = jnp.concatenate([pix[0, at, :], pix[1, at, :], pix[2, at, :]], axis=0)
        for s in range(4):
            ft[g, s * 48 : (s + 1) * 48, :] = dot(xg, permi[s]).astype(BF)
        return carry

    lax.fori_loop(0, 8, flat_body, 0, unroll=8)

    out_copy(1).wait_recv()
    own(0)
    ret[:, mine] = rets[0, :, 0:128]
    back_copy(0, 1).start()

    def own_body(j, carry):
        for half in range(2):
            k = 2 * j + half
            lanes = slice(half * 128, (half + 1) * 128)
            remote(sbuf.at[0], rbuf.at[j, :, lanes], a_s.at[k], a_r.at[k], col_peer(k)).wait_recv()
        own(j)
        for half in range(2):
            back_copy(j, half).start()
        return carry

    lax.fori_loop(1, COLS // 2, own_body, 0)
    for k in range(1, COLS):
        out_copy(k).wait_send()
    for k in range(1, COLS):
        back_copy(k // 2, k % 2).wait_recv()
    eg = dot(ret[...], pmt[...], NT).astype(BF)
    egt = dot(pmt[...], ret[...], NT).astype(BF)

    def make_sum(g, r1, p2, r2, p3, ga, s1, t1, s2, t2, s3, t3):
        first = [
            remote(g.at[col_peer(k)[1]], r1.at[k], s1.at[k], t1.at[k], col_peer(k)) for k in range(1, COLS)
        ]
        second = [remote(p2, r2.at[row], s2.at[k], t2.at[k], row_peer(k)) for k in range(1, ROWS)]
        third = [remote(p3, ga.at[col], s3.at[k], t3.at[k], col_peer(k)) for k in range(1, COLS)]

        def start():
            for cp in first:
                cp.start()

        def turn():
            for cp in first:
                cp.wait_recv()
            total = g[col].astype(F32)
            for k in range(1, COLS):
                total = total + r1[k].astype(F32)
            p2[...] = total.astype(p2.dtype)
            r2[row] = total.astype(p2.dtype)
            for cp in second:
                cp.start()

        def spread():
            for cp in second:
                cp.wait_recv()
            total = r2[0].astype(F32)
            for k in range(1, ROWS):
                total = total + r2[k].astype(F32)
            p3[...] = total.astype(p3.dtype)
            ga[col] = total.astype(p3.dtype)
            for cp in third:
                cp.start()

        def finish():
            for cp in third:
                cp.wait_recv()

        def drain():
            for cp in first + second + third:
                cp.wait_send()

        return start, turn, spread, finish, drain

    start1, turn1, spread1, finish1, drain1 = make_sum(
        g1, g1r1, g1p2, g1r2, g1p3, g1a, p1_s, p1_r, p2_s, p2_r, p3_s, p3_r
    )
    start2, turn2, spread2, finish2, drain2 = make_sum(
        g2, g2r1, g2p2, g2r2, g2p3, g2a, q1_s, q1_r, q2_s, q2_r, q3_s, q3_r
    )
    tap_rows = [remote(g4a, g4r.at[row], t1_s.at[k], t1_r.at[k], row_peer(k)) for k in range(1, ROWS)]
    tap_cols = [remote(g4b, g4c.at[col], t2_s.at[k], t2_r.at[k], col_peer(k)) for k in range(1, COLS)]
    stem_rows = [remote(g3a, g3r.at[row], r1_s.at[k], r1_r.at[k], row_peer(k)) for k in range(1, ROWS)]
    core = lax.rem(col, 2)
    half = (col - core) // 2
    stem_pair = remote(g3s, g3t, r0_s.at[0], r0_r.at[0], (row, col + 1 - 2 * core))
    stem_cols = [
        remote(g3b, g3c.at[half], r2_s.at[k], r2_r.at[k], (row, lax.rem(col + 2 * k, COLS))) for k in range(1, COLS // 2)
    ]

    for b in range(4):
        lanes = slice(b * 128, (b + 1) * 128)
        part = dot(eg, gp[:, lanes]).astype(BF)
        for n in range(4):
            g1[4 * b + n] = part[n * 48 : (n + 1) * 48]
    start1()

    gb = dot(egt, dwt[...])
    for i in range(16):
        for b in range(4):
            gs[2 * i + b // 2, pl.ds(b % 2, 32, stride=2), :] = gb[i * 32 : (i + 1) * 32, b * 128 : (b + 1) * 128]

    acc_e[...] = jnp.zeros_like(acc_e)
    acc_r[...] = jnp.zeros_like(acc_r)

    def back_body(b, carry):
        rows4 = pl.ds(b * 4, 4)
        rows = pl.ds(pl.multiple_of(b * 256, 256), 256)
        grad = gs[rows4].reshape(256, 128)
        grad = norm_back_lanes(dn[rows4].reshape(256, 128), ds[rows, :], grad) * mask
        gs[rows4] = grad.reshape(4, 64, 128)
        og = grad.astype(BF)
        acc_r[...] += dot(og, act[rows, :], TN)
        hid = (dot(og, wr128[...]) * slope[rows, :].astype(F32)).astype(BF)
        acc_e[...] += dot(mb[rows, :], hid, TN)
        mg = dot(hid, we128[...], NT)
        dg = norm_back_lanes(mn[rows, :], ms[rows, :], mg) * mask
        dgu[rows4] = dg.reshape(4, 64, 128)
        return carry

    lax.fori_loop(0, 8, back_body, 0, unroll=8)

    h_src = (
        dgu.at[0:3], dgu.at[29:32], dgu.at[:, 0:8, :], dgu.at[:, 56:64, :],
        dgu.at[0:3, 0:8, :], dgu.at[0:3, 56:64, :], dgu.at[29:32, 0:8, :], dgu.at[29:32, 56:64, :],
    )
    h_dst = (
        hrow.at[1], hrow.at[0], hcol.at[1], hcol.at[0], hcor.at[3], hcor.at[2], hcor.at[1], hcor.at[0],
    )
    halo = [remote(h_src[n], h_dst[n], h_s.at[n], h_r.at[n], near(n)) for n in range(8)]
    for n in range(8):
        halo[n].start()

    turn1()
    for b in range(3):
        lanes = slice(b * 128, (b + 1) * 128)
        for n in range(2):
            g2[2 * b + n] = acc_e[n * 48 : (n + 1) * 48, lanes].astype(BF)
            g2[6 + 2 * b + n] = acc_r[n * 48 : (n + 1) * 48, lanes].astype(BF)
    for n in range(12, 16):
        g2[n] = jnp.zeros((48, 128), BF)
    start2()

    kt[...] = jnp.zeros_like(kt)
    for v in range(7):

        def taps_body(jb, acc, v=v):
            acc = list(acc)
            here = pl.ds(pl.multiple_of(jb * 8, 8), 8)
            grads = {}
            for r in range(38):
                x = pad[r + 1, pl.ds(jb * 8 + v, 8), :]
                if r < 32:
                    grads[r] = dgu[r, here, :]
                for u in range(7):
                    if 0 <= r - u < 32:
                        acc[u] = acc[u] + grads[r - u] * x
            return tuple(acc)

        sums = lax.fori_loop(0, 8, taps_body, tuple(jnp.zeros((8, 128), F32) for _ in range(7)))
        for u in range(7):
            kt[7 * u + v : 7 * u + v + 1, :] = jnp.sum(sums[u], axis=0, keepdims=True)
    g4a[...] = kt[...].astype(BF)
    g4r[row] = kt[...].astype(BF)
    for cp in tap_rows:
        cp.start()
    spread1()

    for i in range(32):
        dgp[4 + i, 3:67, :] = dgu[i]
    depthwise(dgp, kb, conv, True, 12, lambda n: (1 + n // 6, 1 + n % 6))
    for n in range(8):
        halo[n].wait_recv()
    top, bottom = jnp.where(row > 0, 1.0, 0.0), jnp.where(row < ROWS - 1, 1.0, 0.0)
    left, right = jnp.where(col > 0, 1.0, 0.0), jnp.where(col < COLS - 1, 1.0, 0.0)
    for i in range(3):
        dgp[1 + i, 3:67, :] = hrow[0, i] * top
        dgp[36 + i, 3:67, :] = hrow[1, i] * bottom
        dgp[1 + i, 0:3, :] = hcor[0, i, 5:8] * (top * left)
        dgp[1 + i, 67:70, :] = hcor[1, i, 0:3] * (top * right)
        dgp[36 + i, 0:3, :] = hcor[2, i, 5:8] * (bottom * left)
        dgp[36 + i, 67:70, :] = hcor[3, i, 0:3] * (bottom * right)
    dgp[4:36, 0:3, :] = hcol[0, :, 5:8, :] * left
    dgp[4:36, 67:70, :] = hcol[1, :, 0:3, :] * right

    turn2()
    depthwise(dgp, kb, conv, True, 16, lambda n: ((n // 8) * 3, n % 8))
    depthwise(dgp, kb, conv, True, 4, lambda n: (1 + n // 2, (n % 2) * 7))
    for cp in tap_rows:
        cp.wait_recv()
    total = g4r[0].astype(F32)
    for k in range(1, ROWS):
        total = total + g4r[k].astype(F32)
    g4b[...] = total.astype(BF)
    g4c[col] = total.astype(BF)
    for cp in tap_cols:
        cp.start()
    spread2()

    acc_s[...] = jnp.zeros_like(acc_s)

    def stem_back(g, carry):
        parts = []
        for i in range(4):
            grad = gs[4 * g + i] + conv[4 * g + i]
            parts.append(
                norm_back_lanes(sn[4 * g + i], ss[4 * g + i], grad).astype(BF)
            )
        grads = jnp.concatenate(parts, axis=1)
        for s in range(4):
            acc_s[s * 48 : (s + 1) * 48, :] += dot(ft[g, s * 48 : (s + 1) * 48, :], grads)
        return carry

    lax.fori_loop(0, 8, stem_back, 0, unroll=4)
    rows = iota((192, 128), 0)
    folded = jnp.zeros((192, 128), F32)
    for i4 in range(4):
        folded = folded + jnp.where((rows // 4) % 4 == i4, acc_s[:, i4 * 128 : (i4 + 1) * 128], 0.0)
    m48, q192 = iota((48, 192), 0), iota((48, 192), 1)
    rem = q192 % 48
    gather = (m48 == (rem // 16) * 16 + (rem % 4) * 4 + q192 // 48).astype(F32)
    stem = lax.dot_general(gather, folded, NN, precision=lax.Precision.HIGHEST, preferred_element_type=F32)
    g3s[...] = stem.astype(BF)
    stem_pair.start()
    stem_pair.wait_recv()
    stem = (g3s[...].astype(F32) + g3t[...].astype(F32)).astype(BF)
    g3a[...] = stem
    g3r[row] = stem
    for cp in stem_rows:
        cp.start()
    finish1()
    for b in range(4):
        for n in range(4):
            out_down[n * 48 : (n + 1) * 48, b * C0 : (b + 1) * C0] = g1a[4 * b + n, :, 0:C0].astype(F32)
    for cp in stem_rows:
        cp.wait_recv()
    total = g3r[0].astype(F32)
    for k in range(1, ROWS):
        total = total + g3r[k].astype(F32)
    g3b[...] = total.astype(BF)
    g3c[half] = total.astype(BF)
    for cp in stem_cols:
        cp.start()

    for b in range(6):
        lanes = slice(b * 128, (b + 1) * 128)
        part = dot(nball[0], pgall[0, lanes, :], NT)
        for j in range(1, COLS // 2):
            part = part + dot(nball[j], pgall[j, lanes, :], NT)
        out_owner[0, 0, :, lanes] = part

    finish2()
    for b in range(3):
        lanes = slice(b * 128, (b + 1) * 128)
        for n in range(2):
            at = slice(n * 48, (n + 1) * 48)
            out_expand[at, lanes] = g2a[2 * b + n].astype(F32)
            out_reduce[at, lanes] = g2a[6 + 2 * b + n].astype(F32)
    for cp in tap_cols:
        cp.wait_recv()
    total = g4c[0].astype(F32)
    for k in range(1, COLS):
        total = total + g4c[k].astype(F32)
    out_taps[...] = total[0:49, 0:C0]
    for cp in stem_cols:
        cp.wait_recv()
    total = g3c[0].astype(F32)
    for k in range(1, COLS // 2):
        total = total + g3c[k].astype(F32)
    out_stem[...] = total[:, 0:C0]

    for n in range(8):
        px[n].wait_send()
        halo[n].wait_send()
    for k in range(1, COLS):
        back_copy(k // 2, k % 2).wait_send()
    drain1()
    drain2()
    for cp in [stem_pair] + stem_rows + stem_cols + tap_rows + tap_cols:
        cp.wait_send()


def hand_over(*refs):
    for n in range(6):
        refs[6 + n][...] = refs[n][...].astype(F32)


def on_device(pixels, ws, dk, we, wr, wd, wo, tissue, owners, cot):
    vmem = pl.BlockSpec(memory_space=pltpu.VMEM)
    smem = pl.BlockSpec(memory_space=pltpu.SMEM)
    dma = pltpu.SemaphoreType.DMA
    V = pltpu.VMEM
    outs = ((48, C0), (49, C0), (C0, HID), (C0, HID), (C1, 4 * C0), (1, 1, C1, E))
    results = pl.pallas_call(
        kernel,
        out_shape=tuple(jax.ShapeDtypeStruct(s, F32) for s in outs),
        in_specs=[vmem] * 7 + [smem, smem, vmem],
        out_specs=(vmem,) * 6,
        scratch_shapes=[
            V((3, 160, 512), BF), V((256, 256), BF), V((2, 32, 128), BF), V((4, 256, 64), BF), V((4, 48, 512), BF), V((48, 128), BF),
            V((49, 8, 128), F32), V((128, HID), BF), V((128, HID), BF), V((C1, 512), BF),
            V((40, 72, 128), F32), V((32, 64, 128), F32), V((32, 64, 128), F32), V((8, 192, 64), BF),
            V((32, 64, 128), F32), V((2048, 128), F32), V((2048, 128), F32), V((2048, 128), BF),
            V((2048, HID), BF), V((2048, HID), BF), V((32, 64, 128), F32), V((2048, 128), F32),
            V((512, 512), BF), V((512, 2048), BF),
            V((16, E), F32), V((16, 208, 128), BF), V((8, 208, 256), BF), V((8, C1, 256), BF), V((C1, 2048), BF),
            V((8, C1, 256), BF), V((8, E, 256), BF),
            V((E, C1), BF), V((32, 64, 128), F32), V((32, 64, 128), F32), V((40, 72, 128), F32),
            V((2, 3, 64, 128), F32), V((2, 32, 8, 128), F32), V((4, 3, 8, 128), F32),
            V((192, 512), F32), V((128, HID), F32), V((128, HID), F32),
            V((16, 48, 128), BF), V((16, 48, 128), BF), V((48, 128), BF), V((8, 48, 128), BF), V((48, 128), BF),
            V((16, 48, 128), BF),
            V((16, 48, 128), BF), V((16, 48, 128), BF), V((48, 128), BF), V((8, 48, 128), BF), V((48, 128), BF),
            V((16, 48, 128), BF),
            V((64, 128), F32), V((48, 128), BF), V((48, 128), BF), V((48, 128), BF), V((8, 48, 128), BF), V((48, 128), BF),
            V((8, 48, 128), BF),
            V((64, 128), BF), V((8, 64, 128), BF), V((64, 128), BF), V((16, 64, 128), BF),
            dma((8,)), dma((8,)), dma((16,)), dma((16,)), dma((16,)), dma((16,)), dma((8,)), dma((8,)),
            dma((16,)), dma((16,)), dma((8,)), dma((8,)), dma((16,)), dma((16,)),
            dma((16,)), dma((16,)), dma((8,)), dma((8,)), dma((16,)), dma((16,)), dma((8,)), dma((8,)), dma((16,)), dma((16,)),
            dma((1,)), dma((1,)), dma((8,)), dma((8,)), dma((16,)), dma((16,)),
        ],
        compiler_params=pltpu.CompilerParams(
            collective_id=0, has_side_effects=True, vmem_limit_bytes=56 * 1024 * 1024
        ),
    )(pixels, ws, dk.T, we, wr.T, wd.T, wo, tissue, owners.reshape(1, 8), cot)
    stem, taps, expand, reduce, down, owner = pl.pallas_call(
        hand_over,
        out_shape=tuple(jax.ShapeDtypeStruct(s, F32) for s in outs),
        in_specs=[vmem] * 6,
        out_specs=(vmem,) * 6,
    )(*results)
    return stem, taps.T, expand, reduce.T, down.T, owner


def solution(mesh):
    placed = (
        P(None, "row", "col"), P(), P(), P(), P(), P(), P("row", "col", None, None),
        P("row", "col"), P("row", "col", None), P("row", "col", None),
    )
    return jax.shard_map(
        on_device,
        mesh=mesh,
        in_specs=placed,
        out_specs=(P(), P(), P(), P(), P(), P("row", "col", None, None)),
        check_vma=False,
    )
```

```python
import jax
import jax.numpy as jnp
from jax import lax
from jax.experimental import pallas as pl
from jax.experimental.pallas import tpu as pltpu
from jax.sharding import PartitionSpec as P

C0, C1, HID, E = 96, 192, 384, 768
ROWS, COLS = 8, 16
BF, F32, I32 = jnp.bfloat16, jnp.float32, jnp.int32
EPS = 1e-06
SLOPE = 0.7978845608028654
CUBIC = 0.044715
MESH = pl.DeviceIdType.MESH
NEAR = ((-1, 0), (1, 0), (0, -1), (0, 1), (-1, -1), (-1, 1), (1, -1), (1, 1))

NN = (((1,), (0,)), ((), ()))
NT = (((1,), (1,)), ((), ()))
TN = (((0,), (0,)), ((), ()))


def dot(a, b, dims=NN):
    return lax.dot_general(a, b, dims, preferred_element_type=F32)


def iota(shape, dim):
    return lax.broadcasted_iota(I32, shape, dim)


def norm_lanes(x, mask):
    mean = jnp.sum(x, axis=-1, keepdims=True) * (1.0 / C0)
    center = (x - mean) * mask
    scale = lax.rsqrt(jnp.sum(center * center, axis=-1, keepdims=True) * (1.0 / C0) + EPS)
    return center * scale, scale


def norm_back_lanes(normed, scale, grad):
    mean = jnp.sum(grad, axis=-1, keepdims=True) * (1.0 / C0)
    proj = jnp.sum(grad * normed, axis=-1, keepdims=True) * (1.0 / C0)
    return scale * (grad - mean - normed * proj)


def gelu_both(h):
    sq = h * h
    t = jnp.tanh(SLOPE * h * (1.0 + CUBIC * sq))
    half = 0.5 * (1.0 + t)
    return h * half, half + 0.5 * h * (1.0 - t * t) * (SLOPE * (1.0 + 3.0 * CUBIC * sq))


def depthwise(src, kb, dst, flip, count=32, tile=lambda n: (n // 8, n % 8)):
    def body(n, carry):
        ib, jb = tile(n)
        i0 = ib * 8
        acc = [None] * 8
        for v in range(7):
            taps = []
            for u in range(7):
                tap = 7 * u + v
                taps.append(kb[48 - tap if flip else tap])
            for r in range(14):
                x = src[i0 + r + 1, pl.ds(jb * 8 + v, 8), :]
                for u in range(7):
                    i = r - u
                    if 0 <= i < 8:
                        term = taps[u] * x
                        acc[i] = term if acc[i] is None else acc[i] + term
        for i in range(8):
            dst[i0 + i, pl.ds(pl.multiple_of(jb * 8, 8), 8), :] = acc[i]
        return carry

    lax.fori_loop(0, count, body, 0, unroll=2)


def kernel(
    pix, ws, dkt, we, wrt, wdt, wo, tissue, owners, cot,
    out_stem, out_taps, out_expand, out_reduce, out_down, out_owner,
    xe, perm, perms, permi, wblk, ws128, kb, we128, wr128, dwt,
    pad, sn, ss, ft, conv, mn, ms, mb, act, slope, dn, ds, gp, pmt,
    cots, sbuf, rbuf, rets, ret, nball, pgall, wt, gs, dgu, dgp, hsr, hsc, hrow, hcol, hcor,
    acc_s, acc_e, acc_r,
    g1, g1r1, g1p2, g1r2, g1p3, g1a, g2, g2r1, g2p2, g2r2, g2p3, g2a, kt, g3s, g3t, g3a, g3r, g3b, g3c, g4a, g4r, g4b, g4c,
    px_s, px_r, a_s, a_r, b_s, b_r, h_s, h_r,
    p1_s, p1_r, p2_s, p2_r, p3_s, p3_r, q1_s, q1_r, q2_s, q2_r, q3_s, q3_r, r1_s, r1_r, r2_s, r2_r,
    r0_s, r0_r, t1_s, t1_r, t2_s, t2_r,
):
    row, col = lax.axis_index("row"), lax.axis_index("col")

    def near(n):
        dr, dc = NEAR[n]
        return lax.rem(row + (dr + ROWS), ROWS), lax.rem(col + (dc + COLS), COLS)

    def col_peer(k):
        return row, lax.rem(col + k, COLS)

    def row_peer(k):
        return lax.rem(row + k, ROWS), col

    def remote(src, dst, send, recv, dev):
        return pltpu.make_async_remote_copy(
            src_ref=src, dst_ref=dst, send_sem=send, recv_sem=recv, device_id=dev, device_id_type=MESH
        )

    barrier = pltpu.get_barrier_semaphore()
    for k in range(1, COLS):
        pl.semaphore_signal(barrier, inc=1, device_id=col_peer(k), device_id_type=MESH)
    for k in range(1, ROWS):
        pl.semaphore_signal(barrier, inc=1, device_id=row_peer(k), device_id_type=MESH)
    for n in range(4, 8):
        pl.semaphore_signal(barrier, inc=1, device_id=near(n), device_id_type=MESH)
    pl.semaphore_wait(barrier, (COLS - 1) + (ROWS - 1) + 4)

    px_src = (
        pix.at[:, 0:16, :], pix.at[:, 112:128, :], pix.at[:, :, 0:128], pix.at[:, :, 128:256],
        pix.at[:, 0:16, 0:128], pix.at[:, 0:16, 128:256], pix.at[:, 112:128, 0:128], pix.at[:, 112:128, 128:256],
    )
    px_dst = (
        xe.at[:, 144:160, 128:384], xe.at[:, 0:16, 128:384], xe.at[:, 16:144, 384:512], xe.at[:, 16:144, 0:128],
        xe.at[:, 144:160, 384:512], xe.at[:, 144:160, 0:128], xe.at[:, 0:16, 384:512], xe.at[:, 0:16, 0:128],
    )
    px = [remote(px_src[n], px_dst[n], px_s.at[n], px_r.at[n], near(n)) for n in range(8)]
    for n in range(8):
        px[n].start()

    mask = (iota((1, 128), 1) < C0).astype(F32)
    pr = iota((256, 256), 0)
    perm[...] = (iota((256, 256), 1) == 4 * (pr % 64) + pr // 64).astype(F32).astype(BF)
    pr = iota((32, 128), 0)
    pl_ = iota((32, 128), 1)
    perms[0] = jnp.where(pr % 8 < 3, (pl_ == 116 + 4 * (pr % 8) + pr // 8).astype(F32), 0.0).astype(BF)
    perms[1] = jnp.where(pr % 8 < 3, (pl_ == 4 * (pr % 8) + pr // 8).astype(F32), 0.0).astype(BF)
    for s in range(4):
        permi[s] = (iota((256, 64), 0) == 4 * iota((256, 64), 1) + s).astype(F32).astype(BF)
    ws128[...] = jnp.zeros_like(ws128)
    ws128[:, 0:C0] = ws[...]
    q48 = iota((48, 48), 0)
    ql = iota((48, 128), 0)
    for s in range(4):
        pick = (iota((48, 48), 1) == (q48 // 16) * 16 + (q48 % 4) * 4 + s).astype(F32).astype(BF)
        wsel = dot(pick, ws128[...])
        for i4 in range(4):
            wblk[s, :, i4 * 128 : (i4 + 1) * 128] = jnp.where((ql // 4) % 4 == i4, wsel, 0.0).astype(BF)
    kb[...] = jnp.zeros_like(kb)
    for t in range(49):
        kb[t, :, 0:C0] = jnp.broadcast_to(dkt[t : t + 1, :], (8, C0))
    we128[...] = jnp.zeros_like(we128)
    we128[0:C0, :] = we[...]
    wr128[...] = jnp.zeros_like(wr128)
    wr128[0:C0, :] = wrt[...]
    dwt[...] = jnp.zeros_like(dwt)
    for b in range(4):
        dwt[:, b * 128 : b * 128 + C0] = wdt[:, b * C0 : (b + 1) * C0]

    def stem_piece(ref, r0, lanes, chooser, width, use):
        at = pl.ds(pl.multiple_of(r0, 16), 16)
        xg = jnp.concatenate([ref[0, at, lanes], ref[1, at, lanes], ref[2, at, lanes]], axis=0)
        turned = dot(chooser, xg, NT)
        total = jnp.zeros((width, 512), F32)
        for s in range(4):
            total = total + dot(turned[s * width : (s + 1) * width].astype(BF), wblk[s])
        for i4 in range(4):
            use(i4, *norm_lanes(total[:, i4 * 128 : (i4 + 1) * 128], mask))

    def stem_body(g, carry):
        def use(i4, normed, scale):
            pad[4 * g + 4 + i4, 3:67, :] = normed.astype(BF).astype(F32)
            sn[4 * g + i4] = normed
            ss[4 * g + i4] = jnp.broadcast_to(scale, (64, 128))

        stem_piece(pix, g * 16, slice(0, 256), perm[...], 64, use)
        return carry

    lax.fori_loop(0, 8, stem_body, 0, unroll=8)

    slots = []
    for p in range(8):
        rank = 0
        for q in range(p):
            same = jnp.where(owners[0, q] == owners[0, p], 1, 0)
            rank = rank + same * tissue[q // 4, q % 4]
        slots.append(jnp.where(tissue[p // 4, p % 4] == 1, owners[0, p] * 2 + rank, -1000))
    rr = iota((512, 128), 0)
    ll = iota((512, 128), 1)
    patch = (rr // 256) * 4 + (rr % 32) // 8
    slot_row = jnp.zeros((512, 128), I32)
    for p in range(8):
        slot_row = jnp.where(patch == p, slots[p], slot_row)
    hit = jnp.where(((rr // 32) % 8) * 8 + rr % 8 == ll % 64, slot_row - ll // 64, -2000)
    for d in range(COLS):
        pmt[:, d * 128 : (d + 1) * 128] = (hit == 2 * d).astype(F32).astype(BF)
    cots[...] = jnp.zeros_like(cots)
    cots[0:4, :] = cot[0].astype(F32)
    cots[4:8, :] = cot[1].astype(F32)
    slot_lane = jnp.full((256, 16), -1000, I32)
    for p in range(8):
        slot_lane = jnp.where(iota((256, 16), 1) == p, slots[p], slot_lane)
    ro = iota((256, 16), 0)
    rem16 = ro % 16
    want = jnp.where(rem16 < 12, 2 * (ro // 16) + rem16 // 6, -3000)
    packed = jnp.zeros((256, 128), F32)
    for b in range(6):
        choose = jnp.where(rem16 % 6 == b, want, -3000)
        packed = packed + dot(
            (slot_lane == choose).astype(F32).astype(BF), cots[:, b * 128 : (b + 1) * 128].astype(BF)
        )
    for d in range(COLS):
        sbuf[d, C1 : C1 + 16, :] = packed[d * 16 : (d + 1) * 16].astype(BF)

    for n in range(8):
        px[n].wait_recv()

    @pl.when(row == 0)
    def _():
        xe[:, 0:16, :] = jnp.zeros((3, 16, 512), BF)

    @pl.when(row == ROWS - 1)
    def _():
        xe[:, 144:160, :] = jnp.zeros((3, 16, 512), BF)

    @pl.when(col == 0)
    def _():
        xe[:, :, 0:128] = jnp.zeros((3, 160, 128), BF)

    @pl.when(col == COLS - 1)
    def _():
        xe[:, :, 384:512] = jnp.zeros((3, 160, 128), BF)

    def side_body(g, carry):
        for side in range(2):
            def use(i4, normed, scale, side=side):
                pad[4 * g + i4, side * 67 : side * 67 + 3, :] = normed[0:3].astype(BF).astype(F32)

            stem_piece(xe, g * 16, slice(side * 384, side * 384 + 128), perms[side], 8, use)
        return carry

    lax.fori_loop(0, 10, side_body, 0, unroll=10)
    for g in (0, 9):

        def use(i4, normed, scale, g=g):
            pad[4 * g + i4, 3:67, :] = normed.astype(BF).astype(F32)

        stem_piece(xe, g * 16, slice(128, 384), perm[...], 64, use)

    depthwise(pad, kb, conv, False)

    def mlp_body(b, carry):
        rows4 = pl.ds(b * 4, 4)
        rows = pl.ds(pl.multiple_of(b * 256, 256), 256)
        normed, scale = norm_lanes(conv[rows4].reshape(256, 128), mask)
        mn[rows, :] = normed
        ms[rows, :] = jnp.broadcast_to(scale, (256, 128))
        mixed = normed.astype(BF)
        mb[rows, :] = mixed
        value, grad = gelu_both(dot(mixed, we128[...]))
        value = value.astype(BF)
        act[rows, :] = value
        slope[rows, :] = grad.astype(BF)
        block = jnp.concatenate([pad[b * 4 + 4 + i, 3:67, :] for i in range(4)], axis=0)
        block = block + dot(value, wr128[...], NT)
        normed, scale = norm_lanes(block, mask)
        dn[rows4] = normed.reshape(4, 64, 128)
        ds[rows, :] = jnp.broadcast_to(scale, (256, 128))
        return carry

    lax.fori_loop(0, 8, mlp_body, 0, unroll=8)

    def group_body(i, carry):
        rows = pl.ds(pl.multiple_of(i * 32, 32), 32)
        for u in range(2):
            for v in range(2):
                b = 2 * u + v
                gp[rows, b * 128 : (b + 1) * 128] = dn[2 * i + u, pl.ds(v, 32, stride=2), :].astype(BF)
        return carry

    lax.fori_loop(0, 16, group_body, 0)
    embed = dot(dwt[...], gp[...], NT).astype(BF)

    for d in range(COLS):
        sbuf[d, 0:C1, :] = dot(embed, pmt[:, d * 128 : (d + 1) * 128]).astype(BF)
    def out_copy(k):
        peer = col_peer(k)
        lanes = slice((k % 2) * 128, (k % 2 + 1) * 128)
        return remote(sbuf.at[peer[1]], rbuf.at[k // 2, :, lanes], a_s.at[k], a_r.at[k], peer)

    for k in range(1, COLS):
        out_copy(k).start()
    rbuf[0, :, 0:128] = sbuf[col]

    sel = (iota((16, E), 0) == ((iota((16, E), 1) % 128) // 64) * 6 + iota((16, E), 1) // 128).astype(F32).astype(BF)
    cot_scale = (ROWS * COLS) ** (-0.5) / 8.0
    mine = pl.ds(pl.multiple_of(col * 128, 128), 128)

    def back_copy(j, half):
        k = 2 * j + half
        dev = (row, lax.rem(col - k + COLS, COLS))
        lanes = slice(half * 128, (half + 1) * 128)
        return remote(rets.at[j, :, lanes], ret.at[:, mine], b_s.at[k], b_r.at[k], dev)

    def own(j):
        cells = rbuf[j, 0:C1, :].astype(F32)
        mean = jnp.sum(cells, axis=0, keepdims=True) * (1.0 / C1)
        center = cells - mean
        scale = lax.rsqrt(jnp.sum(center * center, axis=0, keepdims=True) * (1.0 / C1) + EPS)
        normed = center * scale
        nb = normed.astype(BF)
        nball[j] = nb
        cots_a = dot(rbuf[j, C1 : C1 + 16, 0:128], sel, TN) * cot_scale
        cots_b = dot(rbuf[j, C1 : C1 + 16, 128:256], sel, TN) * cot_scale
        for b in range(6):
            lanes = slice(b * 128, (b + 1) * 128)
            pre = dot(wt[lanes, :], nb)
            cott = jnp.concatenate([cots_a[:, lanes], cots_b[:, lanes]], axis=1)
            pgall[j, lanes, :] = (cott * gelu_both(pre)[1]).astype(BF)
        back = dot(wo[0, 0], pgall[j])
        mean = jnp.sum(back, axis=0, keepdims=True) * (1.0 / C1)
        proj = jnp.sum(back * normed, axis=0, keepdims=True) * (1.0 / C1)
        rets[j] = (scale * (back - mean - normed * proj)).astype(BF)

    wt[...] = wo[0, 0].astype(F32).T.astype(BF)
    def flat_body(g, carry):
        at = pl.ds(pl.multiple_of(g * 16, 16), 16)
        xg = jnp.concatenate([pix[0, at, :], pix[1, at, :], pix[2, at, :]], axis=0)
        for s in range(4):
            ft[g, s * 48 : (s + 1) * 48, :] = dot(xg, permi[s]).astype(BF)
        return carry

    lax.fori_loop(0, 8, flat_body, 0, unroll=8)

    out_copy(1).wait_recv()
    own(0)
    ret[:, mine] = rets[0, :, 0:128]
    back_copy(0, 1).start()

    def own_body(j, carry):
        for half in range(2):
            k = 2 * j + half
            lanes = slice(half * 128, (half + 1) * 128)
            remote(sbuf.at[0], rbuf.at[j, :, lanes], a_s.at[k], a_r.at[k], col_peer(k)).wait_recv()
        own(j)
        for half in range(2):
            back_copy(j, half).start()
        return carry

    lax.fori_loop(1, COLS // 2, own_body, 0)
    for k in range(1, COLS):
        out_copy(k).wait_send()
    for k in range(1, COLS):
        back_copy(k // 2, k % 2).wait_recv()
    eg = dot(ret[...], pmt[...], NT).astype(BF)
    egt = dot(pmt[...], ret[...], NT).astype(BF)

    def make_sum(g, r1, p2, r2, p3, ga, s1, t1, s2, t2, s3, t3):
        first = [
            remote(g.at[col_peer(k)[1]], r1.at[k], s1.at[k], t1.at[k], col_peer(k)) for k in range(1, COLS)
        ]
        second = [remote(p2, r2.at[row], s2.at[k], t2.at[k], row_peer(k)) for k in range(1, ROWS)]
        third = [remote(p3, ga.at[col], s3.at[k], t3.at[k], col_peer(k)) for k in range(1, COLS)]

        def start():
            for cp in first:
                cp.start()

        def turn():
            for cp in first:
                cp.wait_recv()
            total = g[col].astype(F32)
            for k in range(1, COLS):
                total = total + r1[k].astype(F32)
            p2[...] = total.astype(p2.dtype)
            r2[row] = total.astype(p2.dtype)
            for cp in second:
                cp.start()

        def spread():
            for cp in second:
                cp.wait_recv()
            total = r2[0].astype(F32)
            for k in range(1, ROWS):
                total = total + r2[k].astype(F32)
            p3[...] = total.astype(p3.dtype)
            ga[col] = total.astype(p3.dtype)
            for cp in third:
                cp.start()

        def finish():
            for cp in third:
                cp.wait_recv()

        def drain():
            for cp in first + second + third:
                cp.wait_send()

        return start, turn, spread, finish, drain

    start1, turn1, spread1, finish1, drain1 = make_sum(
        g1, g1r1, g1p2, g1r2, g1p3, g1a, p1_s, p1_r, p2_s, p2_r, p3_s, p3_r
    )
    start2, turn2, spread2, finish2, drain2 = make_sum(
        g2, g2r1, g2p2, g2r2, g2p3, g2a, q1_s, q1_r, q2_s, q2_r, q3_s, q3_r
    )
    tap_rows = [remote(g4a, g4r.at[row], t1_s.at[k], t1_r.at[k], row_peer(k)) for k in range(1, ROWS)]
    tap_cols = [remote(g4b, g4c.at[col], t2_s.at[k], t2_r.at[k], col_peer(k)) for k in range(1, COLS)]
    stem_rows = [remote(g3a, g3r.at[row], r1_s.at[k], r1_r.at[k], row_peer(k)) for k in range(1, ROWS)]
    core = lax.rem(col, 2)
    half = (col - core) // 2
    stem_pair = remote(g3s, g3t, r0_s.at[0], r0_r.at[0], (row, col + 1 - 2 * core))
    stem_cols = [
        remote(g3b, g3c.at[half], r2_s.at[k], r2_r.at[k], (row, lax.rem(col + 2 * k, COLS))) for k in range(1, COLS // 2)
    ]

    for b in range(4):
        lanes = slice(b * 128, (b + 1) * 128)
        part = dot(eg, gp[:, lanes]).astype(BF)
        for n in range(4):
            g1[4 * b + n] = part[n * 48 : (n + 1) * 48]
    start1()

    gb = dot(egt, dwt[...])
    for i in range(16):
        for b in range(4):
            gs[2 * i + b // 2, pl.ds(b % 2, 32, stride=2), :] = gb[i * 32 : (i + 1) * 32, b * 128 : (b + 1) * 128]

    acc_e[...] = jnp.zeros_like(acc_e)
    acc_r[...] = jnp.zeros_like(acc_r)

    def back_body(b, carry):
        rows4 = pl.ds(b * 4, 4)
        rows = pl.ds(pl.multiple_of(b * 256, 256), 256)
        grad = gs[rows4].reshape(256, 128)
        grad = norm_back_lanes(dn[rows4].reshape(256, 128), ds[rows, :], grad) * mask
        gs[rows4] = grad.reshape(4, 64, 128)
        og = grad.astype(BF)
        acc_r[...] += dot(og, act[rows, :], TN)
        hid = (dot(og, wr128[...]) * slope[rows, :].astype(F32)).astype(BF)
        acc_e[...] += dot(mb[rows, :], hid, TN)
        mg = dot(hid, we128[...], NT)
        dg = norm_back_lanes(mn[rows, :], ms[rows, :], mg) * mask
        dgu[rows4] = dg.reshape(4, 64, 128)
        return carry

    lax.fori_loop(0, 8, back_body, 0, unroll=8)

    hsr[0] = dgu[0:3].reshape(192, 128).astype(BF)
    hsr[1] = dgu[29:32].reshape(192, 128).astype(BF)
    for n in range(3):
        hsc[0, n * 32 : (n + 1) * 32, :] = dgu[:, n, :].astype(BF)
        hsc[1, n * 32 : (n + 1) * 32, :] = dgu[:, 61 + n, :].astype(BF)
    h_src = (
        hsr.at[0], hsr.at[1], hsc.at[0], hsc.at[1],
        dgu.at[0:3, 0:8, :], dgu.at[0:3, 56:64, :], dgu.at[29:32, 0:8, :], dgu.at[29:32, 56:64, :],
    )
    h_dst = (
        hrow.at[1], hrow.at[0], hcol.at[1], hcol.at[0], hcor.at[3], hcor.at[2], hcor.at[1], hcor.at[0],
    )
    halo = [remote(h_src[n], h_dst[n], h_s.at[n], h_r.at[n], near(n)) for n in range(8)]
    for n in range(8):
        halo[n].start()

    turn1()
    for b in range(3):
        lanes = slice(b * 128, (b + 1) * 128)
        for n in range(2):
            g2[2 * b + n] = acc_e[n * 48 : (n + 1) * 48, lanes].astype(BF)
            g2[6 + 2 * b + n] = acc_r[n * 48 : (n + 1) * 48, lanes].astype(BF)
    for n in range(12, 16):
        g2[n] = jnp.zeros((48, 128), BF)
    start2()

    kt[...] = jnp.zeros_like(kt)
    for v in range(7):

        def taps_body(jb, acc, v=v):
            acc = list(acc)
            here = pl.ds(pl.multiple_of(jb * 8, 8), 8)
            grads = {}
            for r in range(38):
                x = pad[r + 1, pl.ds(jb * 8 + v, 8), :]
                if r < 32:
                    grads[r] = dgu[r, here, :]
                for u in range(7):
                    if 0 <= r - u < 32:
                        acc[u] = acc[u] + grads[r - u] * x
            return tuple(acc)

        sums = lax.fori_loop(0, 8, taps_body, tuple(jnp.zeros((8, 128), F32) for _ in range(7)))
        for u in range(7):
            kt[7 * u + v : 7 * u + v + 1, :] = jnp.sum(sums[u], axis=0, keepdims=True)
    g4a[...] = kt[...].astype(BF)
    g4r[row] = kt[...].astype(BF)
    for cp in tap_rows:
        cp.start()
    spread1()

    for i in range(32):
        dgp[4 + i, 3:67, :] = dgu[i]
    depthwise(dgp, kb, conv, True, 12, lambda n: (1 + n // 6, 1 + n % 6))
    for n in range(8):
        halo[n].wait_recv()
    top, bottom = jnp.where(row > 0, 1.0, 0.0), jnp.where(row < ROWS - 1, 1.0, 0.0)
    left, right = jnp.where(col > 0, 1.0, 0.0), jnp.where(col < COLS - 1, 1.0, 0.0)
    for i in range(3):
        dgp[1 + i, 3:67, :] = hrow[0, i * 64 : (i + 1) * 64, :].astype(F32) * top
        dgp[36 + i, 3:67, :] = hrow[1, i * 64 : (i + 1) * 64, :].astype(F32) * bottom
        dgp[1 + i, 0:3, :] = hcor[0, i, 5:8] * (top * left)
        dgp[1 + i, 67:70, :] = hcor[1, i, 0:3] * (top * right)
        dgp[36 + i, 0:3, :] = hcor[2, i, 5:8] * (bottom * left)
        dgp[36 + i, 67:70, :] = hcor[3, i, 0:3] * (bottom * right)
    for n in range(3):
        dgp[4:36, n, :] = hcol[0, n * 32 : (n + 1) * 32, :].astype(F32) * left
        dgp[4:36, 67 + n, :] = hcol[1, n * 32 : (n + 1) * 32, :].astype(F32) * right

    turn2()
    depthwise(dgp, kb, conv, True, 16, lambda n: ((n // 8) * 3, n % 8))
    depthwise(dgp, kb, conv, True, 4, lambda n: (1 + n // 2, (n % 2) * 7))
    for cp in tap_rows:
        cp.wait_recv()
    total = g4r[0].astype(F32)
    for k in range(1, ROWS):
        total = total + g4r[k].astype(F32)
    g4b[...] = total.astype(BF)
    g4c[col] = total.astype(BF)
    for cp in tap_cols:
        cp.start()
    spread2()

    acc_s[...] = jnp.zeros_like(acc_s)

    def stem_back(g, carry):
        parts = []
        for i in range(4):
            grad = gs[4 * g + i] + conv[4 * g + i]
            parts.append(
                norm_back_lanes(sn[4 * g + i], ss[4 * g + i], grad).astype(BF)
            )
        grads = jnp.concatenate(parts, axis=1)
        for s in range(4):
            acc_s[s * 48 : (s + 1) * 48, :] += dot(ft[g, s * 48 : (s + 1) * 48, :], grads)
        return carry

    lax.fori_loop(0, 8, stem_back, 0, unroll=4)
    rows = iota((192, 128), 0)
    folded = jnp.zeros((192, 128), F32)
    for i4 in range(4):
        folded = folded + jnp.where((rows // 4) % 4 == i4, acc_s[:, i4 * 128 : (i4 + 1) * 128], 0.0)
    m48, q192 = iota((48, 192), 0), iota((48, 192), 1)
    rem = q192 % 48
    gather = (m48 == (rem // 16) * 16 + (rem % 4) * 4 + q192 // 48).astype(F32)
    stem = lax.dot_general(gather, folded, NN, precision=lax.Precision.HIGHEST, preferred_element_type=F32)
    g3s[...] = stem.astype(BF)
    stem_pair.start()
    stem_pair.wait_recv()
    stem = (g3s[...].astype(F32) + g3t[...].astype(F32)).astype(BF)
    g3a[...] = stem
    g3r[row] = stem
    for cp in stem_rows:
        cp.start()
    finish1()
    for b in range(4):
        for n in range(4):
            out_down[n * 48 : (n + 1) * 48, b * C0 : (b + 1) * C0] = g1a[4 * b + n, :, 0:C0].astype(F32)
    for cp in stem_rows:
        cp.wait_recv()
    total = g3r[0].astype(F32)
    for k in range(1, ROWS):
        total = total + g3r[k].astype(F32)
    g3b[...] = total.astype(BF)
    g3c[half] = total.astype(BF)
    for cp in stem_cols:
        cp.start()

    for b in range(6):
        lanes = slice(b * 128, (b + 1) * 128)
        part = dot(nball[0], pgall[0, lanes, :], NT)
        for j in range(1, COLS // 2):
            part = part + dot(nball[j], pgall[j, lanes, :], NT)
        out_owner[0, 0, :, lanes] = part

    finish2()
    for b in range(3):
        lanes = slice(b * 128, (b + 1) * 128)
        for n in range(2):
            at = slice(n * 48, (n + 1) * 48)
            out_expand[at, lanes] = g2a[2 * b + n].astype(F32)
            out_reduce[at, lanes] = g2a[6 + 2 * b + n].astype(F32)
    for cp in tap_cols:
        cp.wait_recv()
    total = g4c[0].astype(F32)
    for k in range(1, COLS):
        total = total + g4c[k].astype(F32)
    out_taps[...] = total[0:49, 0:C0]
    for cp in stem_cols:
        cp.wait_recv()
    total = g3c[0].astype(F32)
    for k in range(1, COLS // 2):
        total = total + g3c[k].astype(F32)
    out_stem[...] = total[:, 0:C0]

    for n in range(8):
        px[n].wait_send()
        halo[n].wait_send()
    for k in range(1, COLS):
        back_copy(k // 2, k % 2).wait_send()
    drain1()
    drain2()
    for cp in [stem_pair] + stem_rows + stem_cols + tap_rows + tap_cols:
        cp.wait_send()


def hand_over(*refs):
    for n in range(6):
        refs[6 + n][...] = refs[n][...].astype(F32)


def on_device(pixels, ws, dk, we, wr, wd, wo, tissue, owners, cot):
    vmem = pl.BlockSpec(memory_space=pltpu.VMEM)
    smem = pl.BlockSpec(memory_space=pltpu.SMEM)
    dma = pltpu.SemaphoreType.DMA
    V = pltpu.VMEM
    outs = ((48, C0), (49, C0), (C0, HID), (C0, HID), (C1, 4 * C0), (1, 1, C1, E))
    results = pl.pallas_call(
        kernel,
        out_shape=tuple(jax.ShapeDtypeStruct(s, F32) for s in outs),
        in_specs=[vmem] * 7 + [smem, smem, vmem],
        out_specs=(vmem,) * 6,
        scratch_shapes=[
            V((3, 160, 512), BF), V((256, 256), BF), V((2, 32, 128), BF), V((4, 256, 64), BF), V((4, 48, 512), BF), V((48, 128), BF),
            V((49, 8, 128), F32), V((128, HID), BF), V((128, HID), BF), V((C1, 512), BF),
            V((40, 72, 128), F32), V((32, 64, 128), F32), V((32, 64, 128), F32), V((8, 192, 64), BF),
            V((32, 64, 128), F32), V((2048, 128), F32), V((2048, 128), F32), V((2048, 128), BF),
            V((2048, HID), BF), V((2048, HID), BF), V((32, 64, 128), F32), V((2048, 128), F32),
            V((512, 512), BF), V((512, 2048), BF),
            V((16, E), F32), V((16, 208, 128), BF), V((8, 208, 256), BF), V((8, C1, 256), BF), V((C1, 2048), BF),
            V((8, C1, 256), BF), V((8, E, 256), BF),
            V((E, C1), BF), V((32, 64, 128), F32), V((32, 64, 128), F32), V((40, 72, 128), F32),
            V((2, 192, 128), BF), V((2, 96, 128), BF), V((2, 192, 128), BF), V((2, 96, 128), BF), V((4, 3, 8, 128), F32),
            V((192, 512), F32), V((128, HID), F32), V((128, HID), F32),
            V((16, 48, 128), BF), V((16, 48, 128), BF), V((48, 128), BF), V((8, 48, 128), BF), V((48, 128), BF),
            V((16, 48, 128), BF),
            V((16, 48, 128), BF), V((16, 48, 128), BF), V((48, 128), BF), V((8, 48, 128), BF), V((48, 128), BF),
            V((16, 48, 128), BF),
            V((64, 128), F32), V((48, 128), BF), V((48, 128), BF), V((48, 128), BF), V((8, 48, 128), BF), V((48, 128), BF),
            V((8, 48, 128), BF),
            V((64, 128), BF), V((8, 64, 128), BF), V((64, 128), BF), V((16, 64, 128), BF),
            dma((8,)), dma((8,)), dma((16,)), dma((16,)), dma((16,)), dma((16,)), dma((8,)), dma((8,)),
            dma((16,)), dma((16,)), dma((8,)), dma((8,)), dma((16,)), dma((16,)),
            dma((16,)), dma((16,)), dma((8,)), dma((8,)), dma((16,)), dma((16,)), dma((8,)), dma((8,)), dma((16,)), dma((16,)),
            dma((1,)), dma((1,)), dma((8,)), dma((8,)), dma((16,)), dma((16,)),
        ],
        compiler_params=pltpu.CompilerParams(
            collective_id=0, has_side_effects=True, vmem_limit_bytes=56 * 1024 * 1024
        ),
    )(pixels, ws, dk.T, we, wr.T, wd.T, wo, tissue, owners.reshape(1, 8), cot)
    stem, taps, expand, reduce, down, owner = pl.pallas_call(
        hand_over,
        out_shape=tuple(jax.ShapeDtypeStruct(s, F32) for s in outs),
        in_specs=[vmem] * 6,
        out_specs=(vmem,) * 6,
    )(*results)
    return stem, taps.T, expand, reduce.T, down.T, owner


def solution(mesh):
    placed = (
        P(None, "row", "col"), P(), P(), P(), P(), P(), P("row", "col", None, None),
        P("row", "col"), P("row", "col", None), P("row", "col", None),
    )
    return jax.shard_map(
        on_device,
        mesh=mesh,
        in_specs=placed,
        out_specs=(P(), P(), P(), P(), P(), P("row", "col", None, None)),
        check_vma=False,
    )
```

```python
import jax
import jax.numpy as jnp
from jax import lax
from jax.experimental import pallas as pl
from jax.experimental.pallas import tpu as pltpu
from jax.sharding import PartitionSpec as P

C0, C1, HID, E = 96, 192, 384, 768
ROWS, COLS = 8, 16
BF, F32, I32 = jnp.bfloat16, jnp.float32, jnp.int32
EPS = 1e-06
SLOPE = 0.7978845608028654
CUBIC = 0.044715
MESH = pl.DeviceIdType.MESH
NEAR = ((-1, 0), (1, 0), (0, -1), (0, 1), (-1, -1), (-1, 1), (1, -1), (1, 1))

NN = (((1,), (0,)), ((), ()))
NT = (((1,), (1,)), ((), ()))
TN = (((0,), (0,)), ((), ()))


def dot(a, b, dims=NN):
    return lax.dot_general(a, b, dims, preferred_element_type=F32)


def iota(shape, dim):
    return lax.broadcasted_iota(I32, shape, dim)


def norm_lanes(x, mask):
    mean = jnp.sum(x, axis=-1, keepdims=True) * (1.0 / C0)
    center = (x - mean) * mask
    scale = lax.rsqrt(jnp.sum(center * center, axis=-1, keepdims=True) * (1.0 / C0) + EPS)
    return center * scale, scale


def norm_back_lanes(normed, scale, grad):
    mean = jnp.sum(grad, axis=-1, keepdims=True) * (1.0 / C0)
    proj = jnp.sum(grad * normed, axis=-1, keepdims=True) * (1.0 / C0)
    return scale * (grad - mean - normed * proj)


def gelu_both(h):
    sq = h * h
    t = jnp.tanh(SLOPE * h * (1.0 + CUBIC * sq))
    half = 0.5 * (1.0 + t)
    return h * half, half + 0.5 * h * (1.0 - t * t) * (SLOPE * (1.0 + 3.0 * CUBIC * sq))


def depthwise(src, kb, dst, flip, count=32, tile=lambda n: (n // 8, n % 8)):
    def body(n, carry):
        ib, jb = tile(n)
        i0 = ib * 8
        acc = [None] * 8
        for v in range(7):
            taps = []
            for u in range(7):
                tap = 7 * u + v
                taps.append(kb[48 - tap if flip else tap])
            for r in range(14):
                x = src[i0 + r + 1, pl.ds(jb * 8 + v, 8), :]
                for u in range(7):
                    i = r - u
                    if 0 <= i < 8:
                        term = taps[u] * x
                        acc[i] = term if acc[i] is None else acc[i] + term
        for i in range(8):
            dst[i0 + i, pl.ds(pl.multiple_of(jb * 8, 8), 8), :] = acc[i]
        return carry

    lax.fori_loop(0, count, body, 0, unroll=2)


def kernel(
    pix, ws, dkt, we, wrt, wdt, wo, tissue, owners, cot,
    out_stem, out_taps, out_expand, out_reduce, out_down, out_owner,
    xe, perm, perms, permi, wblk, ws128, kb, we128, wr128, dwt,
    pad, sn, ss, ft, conv, mn, ms, mb, act, slope, dn, ds, gp, pmt,
    cots, sbuf, rbuf, rets, ret, nball, pgall, wt, gs, dgu, dgp, hsr, hsc, hrow, hcol, hcor,
    acc_s, acc_e, acc_r,
    g1, g1r1, g1p2, g1r2, g1p3, g1a, g2, g2r1, g2p2, g2r2, g2p3, g2a, kt, g3s, g3t, g3a, g3r, g3b, g3c, g4a, g4r, g4b, g4c,
    px_s, px_r, a_s, a_r, b_s, b_r, h_s, h_r,
    p1_s, p1_r, p2_s, p2_r, p3_s, p3_r, q1_s, q1_r, q2_s, q2_r, q3_s, q3_r, r1_s, r1_r, r2_s, r2_r,
    r0_s, r0_r, t1_s, t1_r, t2_s, t2_r,
):
    row, col = lax.axis_index("row"), lax.axis_index("col")

    def near(n):
        dr, dc = NEAR[n]
        return lax.rem(row + (dr + ROWS), ROWS), lax.rem(col + (dc + COLS), COLS)

    def col_peer(k):
        return row, lax.rem(col + k, COLS)

    def row_peer(k):
        return lax.rem(row + k, ROWS), col

    def remote(src, dst, send, recv, dev):
        return pltpu.make_async_remote_copy(
            src_ref=src, dst_ref=dst, send_sem=send, recv_sem=recv, device_id=dev, device_id_type=MESH
        )

    barrier = pltpu.get_barrier_semaphore()
    for k in range(1, COLS):
        pl.semaphore_signal(barrier, inc=1, device_id=col_peer(k), device_id_type=MESH)
    for k in range(1, ROWS):
        pl.semaphore_signal(barrier, inc=1, device_id=row_peer(k), device_id_type=MESH)
    for n in range(4, 8):
        pl.semaphore_signal(barrier, inc=1, device_id=near(n), device_id_type=MESH)
    pl.semaphore_wait(barrier, (COLS - 1) + (ROWS - 1) + 4)

    px_src = (
        pix.at[:, 0:16, :], pix.at[:, 112:128, :], pix.at[:, 0:64, 0:128], pix.at[:, 0:64, 128:256],
        pix.at[:, 0:16, 0:128], pix.at[:, 0:16, 128:256], pix.at[:, 112:128, 0:128], pix.at[:, 112:128, 128:256],
        pix.at[:, 64:128, 0:128], pix.at[:, 64:128, 128:256],
    )
    px_dst = (
        xe.at[:, 144:160, 128:384], xe.at[:, 0:16, 128:384], xe.at[:, 16:80, 384:512], xe.at[:, 16:80, 0:128],
        xe.at[:, 144:160, 384:512], xe.at[:, 144:160, 0:128], xe.at[:, 0:16, 384:512], xe.at[:, 0:16, 0:128],
        xe.at[:, 80:144, 384:512], xe.at[:, 80:144, 0:128],
    )
    px = [remote(px_src[n], px_dst[n], px_s.at[n], px_r.at[n], near(n if n < 8 else n - 6)) for n in range(10)]
    for n in (2, 3, 8, 9, 0, 1, 4, 5, 6, 7):
        px[n].start()

    mask = (iota((1, 128), 1) < C0).astype(F32)
    pr = iota((256, 256), 0)
    perm[...] = (iota((256, 256), 1) == 4 * (pr % 64) + pr // 64).astype(F32).astype(BF)
    pr = iota((32, 128), 0)
    pl_ = iota((32, 128), 1)
    perms[0] = jnp.where(pr % 8 < 3, (pl_ == 116 + 4 * (pr % 8) + pr // 8).astype(F32), 0.0).astype(BF)
    perms[1] = jnp.where(pr % 8 < 3, (pl_ == 4 * (pr % 8) + pr // 8).astype(F32), 0.0).astype(BF)
    for s in range(4):
        permi[s] = (iota((256, 64), 0) == 4 * iota((256, 64), 1) + s).astype(F32).astype(BF)
    ws128[...] = jnp.zeros_like(ws128)
    ws128[:, 0:C0] = ws[...]
    q48 = iota((48, 48), 0)
    ql = iota((48, 128), 0)
    for s in range(4):
        pick = (iota((48, 48), 1) == (q48 // 16) * 16 + (q48 % 4) * 4 + s).astype(F32).astype(BF)
        wsel = dot(pick, ws128[...])
        for i4 in range(4):
            wblk[s, :, i4 * 128 : (i4 + 1) * 128] = jnp.where((ql // 4) % 4 == i4, wsel, 0.0).astype(BF)
    kb[...] = jnp.zeros_like(kb)
    for t in range(49):
        kb[t, :, 0:C0] = jnp.broadcast_to(dkt[t : t + 1, :], (8, C0))
    we128[...] = jnp.zeros_like(we128)
    we128[0:C0, :] = we[...]
    wr128[...] = jnp.zeros_like(wr128)
    wr128[0:C0, :] = wrt[...]
    dwt[...] = jnp.zeros_like(dwt)
    for b in range(4):
        dwt[:, b * 128 : b * 128 + C0] = wdt[:, b * C0 : (b + 1) * C0]

    def stem_piece(ref, r0, lanes, chooser, width, use):
        at = pl.ds(pl.multiple_of(r0, 16), 16)
        xg = jnp.concatenate([ref[0, at, lanes], ref[1, at, lanes], ref[2, at, lanes]], axis=0)
        turned = dot(chooser, xg, NT)
        total = jnp.zeros((width, 512), F32)
        for s in range(4):
            total = total + dot(turned[s * width : (s + 1) * width].astype(BF), wblk[s])
        for i4 in range(4):
            use(i4, *norm_lanes(total[:, i4 * 128 : (i4 + 1) * 128], mask))

    def stem_body(g, carry):
        def use(i4, normed, scale):
            pad[4 * g + 4 + i4, 3:67, :] = normed.astype(BF).astype(F32)
            sn[4 * g + i4] = normed
            ss[4 * g + i4] = jnp.broadcast_to(scale, (64, 128))

        stem_piece(pix, g * 16, slice(0, 256), perm[...], 64, use)
        return carry

    lax.fori_loop(0, 8, stem_body, 0, unroll=8)

    slots = []
    for p in range(8):
        rank = 0
        for q in range(p):
            same = jnp.where(owners[0, q] == owners[0, p], 1, 0)
            rank = rank + same * tissue[q // 4, q % 4]
        slots.append(jnp.where(tissue[p // 4, p % 4] == 1, owners[0, p] * 2 + rank, -1000))
    rr = iota((512, 128), 0)
    ll = iota((512, 128), 1)
    patch = (rr // 256) * 4 + (rr % 32) // 8
    slot_row = jnp.zeros((512, 128), I32)
    for p in range(8):
        slot_row = jnp.where(patch == p, slots[p], slot_row)
    hit = jnp.where(((rr // 32) % 8) * 8 + rr % 8 == ll % 64, slot_row - ll // 64, -2000)
    for d in range(COLS):
        pmt[:, d * 128 : (d + 1) * 128] = (hit == 2 * d).astype(F32).astype(BF)
    cots[...] = jnp.zeros_like(cots)
    cots[0:4, :] = cot[0].astype(F32)
    cots[4:8, :] = cot[1].astype(F32)
    slot_lane = jnp.full((256, 16), -1000, I32)
    for p in range(8):
        slot_lane = jnp.where(iota((256, 16), 1) == p, slots[p], slot_lane)
    ro = iota((256, 16), 0)
    rem16 = ro % 16
    want = jnp.where(rem16 < 12, 2 * (ro // 16) + rem16 // 6, -3000)
    packed = jnp.zeros((256, 128), F32)
    for b in range(6):
        choose = jnp.where(rem16 % 6 == b, want, -3000)
        packed = packed + dot(
            (slot_lane == choose).astype(F32).astype(BF), cots[:, b * 128 : (b + 1) * 128].astype(BF)
        )
    for d in range(COLS):
        sbuf[d, C1 : C1 + 16, :] = packed[d * 16 : (d + 1) * 16].astype(BF)

    for n in range(10):
        px[n].wait_recv()

    @pl.when(row == 0)
    def _():
        xe[:, 0:16, :] = jnp.zeros((3, 16, 512), BF)

    @pl.when(row == ROWS - 1)
    def _():
        xe[:, 144:160, :] = jnp.zeros((3, 16, 512), BF)

    @pl.when(col == 0)
    def _():
        xe[:, :, 0:128] = jnp.zeros((3, 160, 128), BF)

    @pl.when(col == COLS - 1)
    def _():
        xe[:, :, 384:512] = jnp.zeros((3, 160, 128), BF)

    def side_body(g, carry):
        for side in range(2):
            def use(i4, normed, scale, side=side):
                pad[4 * g + i4, side * 67 : side * 67 + 3, :] = normed[0:3].astype(BF).astype(F32)

            stem_piece(xe, g * 16, slice(side * 384, side * 384 + 128), perms[side], 8, use)
        return carry

    lax.fori_loop(0, 10, side_body, 0, unroll=10)
    for g in (0, 9):

        def use(i4, normed, scale, g=g):
            pad[4 * g + i4, 3:67, :] = normed.astype(BF).astype(F32)

        stem_piece(xe, g * 16, slice(128, 384), perm[...], 64, use)

    depthwise(pad, kb, conv, False)

    def mlp_body(b, carry):
        rows4 = pl.ds(b * 4, 4)
        rows = pl.ds(pl.multiple_of(b * 256, 256), 256)
        normed, scale = norm_lanes(conv[rows4].reshape(256, 128), mask)
        mn[rows, :] = normed
        ms[rows, :] = jnp.broadcast_to(scale, (256, 128))
        mixed = normed.astype(BF)
        mb[rows, :] = mixed
        value, grad = gelu_both(dot(mixed, we128[...]))
        value = value.astype(BF)
        act[rows, :] = value
        slope[rows, :] = grad.astype(BF)
        block = jnp.concatenate([pad[b * 4 + 4 + i, 3:67, :] for i in range(4)], axis=0)
        block = block + dot(value, wr128[...], NT)
        normed, scale = norm_lanes(block, mask)
        dn[rows4] = normed.reshape(4, 64, 128)
        ds[rows, :] = jnp.broadcast_to(scale, (256, 128))
        return carry

    lax.fori_loop(0, 8, mlp_body, 0, unroll=8)

    def group_body(i, carry):
        rows = pl.ds(pl.multiple_of(i * 32, 32), 32)
        for u in range(2):
            for v in range(2):
                b = 2 * u + v
                gp[rows, b * 128 : (b + 1) * 128] = dn[2 * i + u, pl.ds(v, 32, stride=2), :].astype(BF)
        return carry

    lax.fori_loop(0, 16, group_body, 0)
    embed = dot(dwt[...], gp[...], NT).astype(BF)

    for d in range(COLS):
        sbuf[d, 0:C1, :] = dot(embed, pmt[:, d * 128 : (d + 1) * 128]).astype(BF)
    def out_copy(k):
        peer = col_peer(k)
        lanes = slice((k % 2) * 128, (k % 2 + 1) * 128)
        return remote(sbuf.at[peer[1]], rbuf.at[k // 2, :, lanes], a_s.at[k], a_r.at[k], peer)

    for k in range(1, COLS):
        out_copy(k).start()
    rbuf[0, :, 0:128] = sbuf[col]

    sel = (iota((16, E), 0) == ((iota((16, E), 1) % 128) // 64) * 6 + iota((16, E), 1) // 128).astype(F32).astype(BF)
    cot_scale = (ROWS * COLS) ** (-0.5) / 8.0
    mine = pl.ds(pl.multiple_of(col * 128, 128), 128)

    def back_copy(j, half):
        k = 2 * j + half
        dev = (row, lax.rem(col - k + COLS, COLS))
        lanes = slice(half * 128, (half + 1) * 128)
        return remote(rets.at[j, :, lanes], ret.at[:, mine], b_s.at[k], b_r.at[k], dev)

    def own(j):
        cells = rbuf[j, 0:C1, :].astype(F32)
        mean = jnp.sum(cells, axis=0, keepdims=True) * (1.0 / C1)
        center = cells - mean
        scale = lax.rsqrt(jnp.sum(center * center, axis=0, keepdims=True) * (1.0 / C1) + EPS)
        normed = center * scale
        nb = normed.astype(BF)
        nball[j] = nb
        cots_a = dot(rbuf[j, C1 : C1 + 16, 0:128], sel, TN) * cot_scale
        cots_b = dot(rbuf[j, C1 : C1 + 16, 128:256], sel, TN) * cot_scale
        for b in range(6):
            lanes = slice(b * 128, (b + 1) * 128)
            pre = dot(wt[lanes, :], nb)
            cott = jnp.concatenate([cots_a[:, lanes], cots_b[:, lanes]], axis=1)
            pgall[j, lanes, :] = (cott * gelu_both(pre)[1]).astype(BF)
        back = dot(wo[0, 0], pgall[j])
        mean = jnp.sum(back, axis=0, keepdims=True) * (1.0 / C1)
        proj = jnp.sum(back * normed, axis=0, keepdims=True) * (1.0 / C1)
        rets[j] = (scale * (back - mean - normed * proj)).astype(BF)

    wt[...] = wo[0, 0].astype(F32).T.astype(BF)
    def flat_body(g, carry):
        at = pl.ds(pl.multiple_of(g * 16, 16), 16)
        xg = jnp.concatenate([pix[0, at, :], pix[1, at, :], pix[2, at, :]], axis=0)
        for s in range(4):
            ft[g, s * 48 : (s + 1) * 48, :] = dot(xg, permi[s]).astype(BF)
        return carry

    lax.fori_loop(0, 8, flat_body, 0, unroll=8)

    out_copy(1).wait_recv()
    own(0)
    ret[:, mine] = rets[0, :, 0:128]
    back_copy(0, 1).start()

    def own_body(j, carry):
        for half in range(2):
            k = 2 * j + half
            lanes = slice(half * 128, (half + 1) * 128)
            remote(sbuf.at[0], rbuf.at[j, :, lanes], a_s.at[k], a_r.at[k], col_peer(k)).wait_recv()
        own(j)
        for half in range(2):
            back_copy(j, half).start()
        return carry

    lax.fori_loop(1, COLS // 2, own_body, 0)
    for k in range(1, COLS):
        out_copy(k).wait_send()
    for k in range(1, COLS):
        back_copy(k // 2, k % 2).wait_recv()
    eg = dot(ret[...], pmt[...], NT).astype(BF)
    egt = dot(pmt[...], ret[...], NT).astype(BF)

    def make_sum(g, r1, p2, r2, p3, ga, s1, t1, s2, t2, s3, t3):
        first = [
            remote(g.at[col_peer(k)[1]], r1.at[k], s1.at[k], t1.at[k], col_peer(k)) for k in range(1, COLS)
        ]
        second = [remote(p2, r2.at[row], s2.at[k], t2.at[k], row_peer(k)) for k in range(1, ROWS)]
        third = [remote(p3, ga.at[col], s3.at[k], t3.at[k], col_peer(k)) for k in range(1, COLS)]

        def start():
            for cp in first:
                cp.start()

        def turn():
            for cp in first:
                cp.wait_recv()
            total = g[col].astype(F32)
            for k in range(1, COLS):
                total = total + r1[k].astype(F32)
            p2[...] = total.astype(p2.dtype)
            r2[row] = total.astype(p2.dtype)
            for cp in second:
                cp.start()

        def spread():
            for cp in second:
                cp.wait_recv()
            total = r2[0].astype(F32)
            for k in range(1, ROWS):
                total = total + r2[k].astype(F32)
            p3[...] = total.astype(p3.dtype)
            ga[col] = total.astype(p3.dtype)
            for cp in third:
                cp.start()

        def finish():
            for cp in third:
                cp.wait_recv()

        def drain():
            for cp in first + second + third:
                cp.wait_send()

        return start, turn, spread, finish, drain

    start1, turn1, spread1, finish1, drain1 = make_sum(
        g1, g1r1, g1p2, g1r2, g1p3, g1a, p1_s, p1_r, p2_s, p2_r, p3_s, p3_r
    )
    start2, turn2, spread2, finish2, drain2 = make_sum(
        g2, g2r1, g2p2, g2r2, g2p3, g2a, q1_s, q1_r, q2_s, q2_r, q3_s, q3_r
    )
    tap_rows = [remote(g4a, g4r.at[row], t1_s.at[k], t1_r.at[k], row_peer(k)) for k in range(1, ROWS)]
    tap_cols = [remote(g4b, g4c.at[col], t2_s.at[k], t2_r.at[k], col_peer(k)) for k in range(1, COLS)]
    stem_rows = [remote(g3a, g3r.at[row], r1_s.at[k], r1_r.at[k], row_peer(k)) for k in range(1, ROWS)]
    core = lax.rem(col, 2)
    half = (col - core) // 2
    stem_pair = remote(g3s, g3t, r0_s.at[0], r0_r.at[0], (row, col + 1 - 2 * core))
    stem_cols = [
        remote(g3b, g3c.at[half], r2_s.at[k], r2_r.at[k], (row, lax.rem(col + 2 * k, COLS))) for k in range(1, COLS // 2)
    ]

    for b in range(4):
        lanes = slice(b * 128, (b + 1) * 128)
        part = dot(eg, gp[:, lanes]).astype(BF)
        for n in range(4):
            g1[4 * b + n] = part[n * 48 : (n + 1) * 48]
    start1()

    gb = dot(egt, dwt[...])
    for i in range(16):
        for b in range(4):
            gs[2 * i + b // 2, pl.ds(b % 2, 32, stride=2), :] = gb[i * 32 : (i + 1) * 32, b * 128 : (b + 1) * 128]

    acc_e[...] = jnp.zeros_like(acc_e)
    acc_r[...] = jnp.zeros_like(acc_r)

    def back_body(b, carry):
        rows4 = pl.ds(b * 4, 4)
        rows = pl.ds(pl.multiple_of(b * 256, 256), 256)
        grad = gs[rows4].reshape(256, 128)
        grad = norm_back_lanes(dn[rows4].reshape(256, 128), ds[rows, :], grad) * mask
        gs[rows4] = grad.reshape(4, 64, 128)
        og = grad.astype(BF)
        acc_r[...] += dot(og, act[rows, :], TN)
        hid = (dot(og, wr128[...]) * slope[rows, :].astype(F32)).astype(BF)
        acc_e[...] += dot(mb[rows, :], hid, TN)
        mg = dot(hid, we128[...], NT)
        dg = norm_back_lanes(mn[rows, :], ms[rows, :], mg) * mask
        dgu[rows4] = dg.reshape(4, 64, 128)
        return carry

    lax.fori_loop(0, 8, back_body, 0, unroll=8)

    hsr[0] = dgu[0:3].reshape(192, 128).astype(BF)
    hsr[1] = dgu[29:32].reshape(192, 128).astype(BF)
    for n in range(3):
        hsc[0, n * 32 : (n + 1) * 32, :] = dgu[:, n, :].astype(BF)
        hsc[1, n * 32 : (n + 1) * 32, :] = dgu[:, 61 + n, :].astype(BF)
    h_src = (
        hsr.at[0], hsr.at[1], hsc.at[0], hsc.at[1],
        dgu.at[0:3, 0:8, :], dgu.at[0:3, 56:64, :], dgu.at[29:32, 0:8, :], dgu.at[29:32, 56:64, :],
    )
    h_dst = (
        hrow.at[1], hrow.at[0], hcol.at[1], hcol.at[0], hcor.at[3], hcor.at[2], hcor.at[1], hcor.at[0],
    )
    halo = [remote(h_src[n], h_dst[n], h_s.at[n], h_r.at[n], near(n)) for n in range(8)]
    for n in range(8):
        halo[n].start()

    turn1()
    for b in range(3):
        lanes = slice(b * 128, (b + 1) * 128)
        for n in range(2):
            g2[2 * b + n] = acc_e[n * 48 : (n + 1) * 48, lanes].astype(BF)
            g2[6 + 2 * b + n] = acc_r[n * 48 : (n + 1) * 48, lanes].astype(BF)
    for n in range(12, 16):
        g2[n] = jnp.zeros((48, 128), BF)
    start2()

    kt[...] = jnp.zeros_like(kt)
    for v in range(7):

        def taps_body(jb, acc, v=v):
            acc = list(acc)
            here = pl.ds(pl.multiple_of(jb * 8, 8), 8)
            grads = {}
            for r in range(38):
                x = pad[r + 1, pl.ds(jb * 8 + v, 8), :]
                if r < 32:
                    grads[r] = dgu[r, here, :]
                for u in range(7):
                    if 0 <= r - u < 32:
                        acc[u] = acc[u] + grads[r - u] * x
            return tuple(acc)

        sums = lax.fori_loop(0, 8, taps_body, tuple(jnp.zeros((8, 128), F32) for _ in range(7)))
        for u in range(7):
            kt[7 * u + v : 7 * u + v + 1, :] = jnp.sum(sums[u], axis=0, keepdims=True)
    g4a[...] = kt[...].astype(BF)
    g4r[row] = kt[...].astype(BF)
    for cp in tap_rows:
        cp.start()
    spread1()

    for i in range(32):
        dgp[4 + i, 3:67, :] = dgu[i]
    depthwise(dgp, kb, conv, True, 12, lambda n: (1 + n // 6, 1 + n % 6))
    for n in range(8):
        halo[n].wait_recv()
    top, bottom = jnp.where(row > 0, 1.0, 0.0), jnp.where(row < ROWS - 1, 1.0, 0.0)
    left, right = jnp.where(col > 0, 1.0, 0.0), jnp.where(col < COLS - 1, 1.0, 0.0)
    for i in range(3):
        dgp[1 + i, 3:67, :] = hrow[0, i * 64 : (i + 1) * 64, :].astype(F32) * top
        dgp[36 + i, 3:67, :] = hrow[1, i * 64 : (i + 1) * 64, :].astype(F32) * bottom
        dgp[1 + i, 0:3, :] = hcor[0, i, 5:8] * (top * left)
        dgp[1 + i, 67:70, :] = hcor[1, i, 0:3] * (top * right)
        dgp[36 + i, 0:3, :] = hcor[2, i, 5:8] * (bottom * left)
        dgp[36 + i, 67:70, :] = hcor[3, i, 0:3] * (bottom * right)
    for n in range(3):
        dgp[4:36, n, :] = hcol[0, n * 32 : (n + 1) * 32, :].astype(F32) * left
        dgp[4:36, 67 + n, :] = hcol[1, n * 32 : (n + 1) * 32, :].astype(F32) * right

    turn2()
    depthwise(dgp, kb, conv, True, 16, lambda n: ((n // 8) * 3, n % 8))
    depthwise(dgp, kb, conv, True, 4, lambda n: (1 + n // 2, (n % 2) * 7))
    for cp in tap_rows:
        cp.wait_recv()
    total = g4r[0].astype(F32)
    for k in range(1, ROWS):
        total = total + g4r[k].astype(F32)
    g4b[...] = total.astype(BF)
    g4c[col] = total.astype(BF)
    for cp in tap_cols:
        cp.start()
    spread2()

    acc_s[...] = jnp.zeros_like(acc_s)

    def stem_back(g, carry):
        parts = []
        for i in range(4):
            grad = gs[4 * g + i] + conv[4 * g + i]
            parts.append(
                norm_back_lanes(sn[4 * g + i], ss[4 * g + i], grad).astype(BF)
            )
        grads = jnp.concatenate(parts, axis=1)
        for s in range(4):
            acc_s[s * 48 : (s + 1) * 48, :] += dot(ft[g, s * 48 : (s + 1) * 48, :], grads)
        return carry

    lax.fori_loop(0, 8, stem_back, 0, unroll=4)
    rows = iota((192, 128), 0)
    folded = jnp.zeros((192, 128), F32)
    for i4 in range(4):
        folded = folded + jnp.where((rows // 4) % 4 == i4, acc_s[:, i4 * 128 : (i4 + 1) * 128], 0.0)
    m48, q192 = iota((48, 192), 0), iota((48, 192), 1)
    rem = q192 % 48
    gather = (m48 == (rem // 16) * 16 + (rem % 4) * 4 + q192 // 48).astype(F32)
    stem = lax.dot_general(gather, folded, NN, precision=lax.Precision.HIGHEST, preferred_element_type=F32)
    g3s[...] = stem.astype(BF)
    stem_pair.start()
    stem_pair.wait_recv()
    stem = (g3s[...].astype(F32) + g3t[...].astype(F32)).astype(BF)
    g3a[...] = stem
    g3r[row] = stem
    for cp in stem_rows:
        cp.start()
    finish1()
    for b in range(4):
        for n in range(4):
            out_down[n * 48 : (n + 1) * 48, b * C0 : (b + 1) * C0] = g1a[4 * b + n, :, 0:C0].astype(F32)
    for cp in stem_rows:
        cp.wait_recv()
    total = g3r[0].astype(F32)
    for k in range(1, ROWS):
        total = total + g3r[k].astype(F32)
    g3b[...] = total.astype(BF)
    g3c[half] = total.astype(BF)
    for cp in stem_cols:
        cp.start()

    for b in range(6):
        lanes = slice(b * 128, (b + 1) * 128)
        part = dot(nball[0], pgall[0, lanes, :], NT)
        for j in range(1, COLS // 2):
            part = part + dot(nball[j], pgall[j, lanes, :], NT)
        out_owner[0, 0, :, lanes] = part

    finish2()
    for b in range(3):
        lanes = slice(b * 128, (b + 1) * 128)
        for n in range(2):
            at = slice(n * 48, (n + 1) * 48)
            out_expand[at, lanes] = g2a[2 * b + n].astype(F32)
            out_reduce[at, lanes] = g2a[6 + 2 * b + n].astype(F32)
    for cp in tap_cols:
        cp.wait_recv()
    total = g4c[0].astype(F32)
    for k in range(1, COLS):
        total = total + g4c[k].astype(F32)
    out_taps[...] = total[0:49, 0:C0]
    for cp in stem_cols:
        cp.wait_recv()
    total = g3c[0].astype(F32)
    for k in range(1, COLS // 2):
        total = total + g3c[k].astype(F32)
    out_stem[...] = total[:, 0:C0]

    for n in range(10):
        px[n].wait_send()
    for n in range(8):
        halo[n].wait_send()
    for k in range(1, COLS):
        back_copy(k // 2, k % 2).wait_send()
    drain1()
    drain2()
    for cp in [stem_pair] + stem_rows + stem_cols + tap_rows + tap_cols:
        cp.wait_send()


def hand_over(*refs):
    for n in range(6):
        refs[6 + n][...] = refs[n][...].astype(F32)


def on_device(pixels, ws, dk, we, wr, wd, wo, tissue, owners, cot):
    vmem = pl.BlockSpec(memory_space=pltpu.VMEM)
    smem = pl.BlockSpec(memory_space=pltpu.SMEM)
    dma = pltpu.SemaphoreType.DMA
    V = pltpu.VMEM
    outs = ((48, C0), (49, C0), (C0, HID), (C0, HID), (C1, 4 * C0), (1, 1, C1, E))
    results = pl.pallas_call(
        kernel,
        out_shape=tuple(jax.ShapeDtypeStruct(s, F32) for s in outs),
        in_specs=[vmem] * 7 + [smem, smem, vmem],
        out_specs=(vmem,) * 6,
        scratch_shapes=[
            V((3, 160, 512), BF), V((256, 256), BF), V((2, 32, 128), BF), V((4, 256, 64), BF), V((4, 48, 512), BF), V((48, 128), BF),
            V((49, 8, 128), F32), V((128, HID), BF), V((128, HID), BF), V((C1, 512), BF),
            V((40, 72, 128), F32), V((32, 64, 128), F32), V((32, 64, 128), F32), V((8, 192, 64), BF),
            V((32, 64, 128), F32), V((2048, 128), F32), V((2048, 128), F32), V((2048, 128), BF),
            V((2048, HID), BF), V((2048, HID), BF), V((32, 64, 128), F32), V((2048, 128), F32),
            V((512, 512), BF), V((512, 2048), BF),
            V((16, E), F32), V((16, 208, 128), BF), V((8, 208, 256), BF), V((8, C1, 256), BF), V((C1, 2048), BF),
            V((8, C1, 256), BF), V((8, E, 256), BF),
            V((E, C1), BF), V((32, 64, 128), F32), V((32, 64, 128), F32), V((40, 72, 128), F32),
            V((2, 192, 128), BF), V((2, 96, 128), BF), V((2, 192, 128), BF), V((2, 96, 128), BF), V((4, 3, 8, 128), F32),
            V((192, 512), F32), V((128, HID), F32), V((128, HID), F32),
            V((16, 48, 128), BF), V((16, 48, 128), BF), V((48, 128), BF), V((8, 48, 128), BF), V((48, 128), BF),
            V((16, 48, 128), BF),
            V((16, 48, 128), BF), V((16, 48, 128), BF), V((48, 128), BF), V((8, 48, 128), BF), V((48, 128), BF),
            V((16, 48, 128), BF),
            V((64, 128), F32), V((48, 128), BF), V((48, 128), BF), V((48, 128), BF), V((8, 48, 128), BF), V((48, 128), BF),
            V((8, 48, 128), BF),
            V((64, 128), BF), V((8, 64, 128), BF), V((64, 128), BF), V((16, 64, 128), BF),
            dma((10,)), dma((10,)), dma((16,)), dma((16,)), dma((16,)), dma((16,)), dma((8,)), dma((8,)),
            dma((16,)), dma((16,)), dma((8,)), dma((8,)), dma((16,)), dma((16,)),
            dma((16,)), dma((16,)), dma((8,)), dma((8,)), dma((16,)), dma((16,)), dma((8,)), dma((8,)), dma((16,)), dma((16,)),
            dma((1,)), dma((1,)), dma((8,)), dma((8,)), dma((16,)), dma((16,)),
        ],
        compiler_params=pltpu.CompilerParams(
            collective_id=0, has_side_effects=True, vmem_limit_bytes=56 * 1024 * 1024
        ),
    )(pixels, ws, dk.T, we, wr.T, wd.T, wo, tissue, owners.reshape(1, 8), cot)
    stem, taps, expand, reduce, down, owner = pl.pallas_call(
        hand_over,
        out_shape=tuple(jax.ShapeDtypeStruct(s, F32) for s in outs),
        in_specs=[vmem] * 6,
        out_specs=(vmem,) * 6,
    )(*results)
    return stem, taps.T, expand, reduce.T, down.T, owner


def solution(mesh):
    placed = (
        P(None, "row", "col"), P(), P(), P(), P(), P(), P("row", "col", None, None),
        P("row", "col"), P("row", "col", None), P("row", "col", None),
    )
    return jax.shard_map(
        on_device,
        mesh=mesh,
        in_specs=placed,
        out_specs=(P(), P(), P(), P(), P(), P("row", "col", None, None)),
        check_vma=False,
    )
```
